32 devices in a mesh: ctx: 8 (over z, core), dp: 4 (over y, x).
Axes of the slice: x: 2, y: 2, z: 4, core: 2. Of those that a mesh axis runs over, the one named last changes fastest.
Arguments:
- query: bfloat16 [8, 8, 64, 2048], P('ctx', 'dp'), parts along dimension 1, may hold values from -21 to 21
- key: bfloat16 [8, 8, 64, 256], P('ctx', 'dp'), parts along dimension 1, may hold values from -21 to 21
- value: bfloat16 [8, 8, 64, 256], P('ctx', 'dp'), parts along dimension 1, may hold values from -6 to 6
- out_grad: bfloat16 [8, 8, 64, 2048], P('ctx', 'dp'), parts along dimension 1, may hold values from -6 to 6
- attn_out: bfloat16 [8, 8, 64, 2048], P('ctx', 'dp'), parts along dimension 1, may hold values from -4 to 4
- doc_start: int32 [8, 8, 64], P('ctx', 'dp'), parts along dimension 1, may hold values from 0 to 1023, as said below
Outputs:
- q_grad: bfloat16 [8, 8, 64, 2048], P('ctx', 'dp'), parts along dimension 1
- k_grad: bfloat16 [8, 8, 64, 256], P('ctx', 'dp'), parts along dimension 1
- v_grad: bfloat16 [8, 8, 64, 256], P('ctx', 'dp'), parts along dimension 1
The draws below stay inside these ranges and needn't reach their ends.
There are 4 independent parts, one for each index of `dp`. The reference program is written for one: setup_inputs(seed, part) draws one part's arguments, and reference() takes and returns one part's arrays. A program takes and returns all parts, laid end to end along the dimension named above; each array names one. Nothing has to cross between parts.
Inputs may be any that keep to these rules, and one draw needn't show every extreme that they name: Documents are runs of consecutive positions and doc_start(i) is the first position of the document that holds token i, so doc_start never falls along the sequence and doc_start(i) <= i.
All inputs are finite; a program needn't handle non-finite values.
Results may differ from the reference program's by a relative error of at most 0.0085.
Values may be sent and summed in bfloat16 or wider, within the bound.
No kernel may reach another device: no remote copies, remote signals or barrier semaphores. Data moves between devices by JAX's collectives and lax.ppermute only.
A program may use at most 64 MiB of HBM per device.

```python
import jax
import jax.numpy as jnp
from jax import lax

HEAD_SIZE = 128
QUERY_PER_KV = 8
KEY_VALUE_HEADS = 2
HQ = 16
STEPS = 4
BLOCK_TOKENS = 64
WIN = 256
TOKENS = 1024
N_CTX = 8


def to_storage(sequence):
    half_count = sequence.shape[0] // 2
    return jnp.stack([sequence[:half_count], sequence[half_count:][::-1]], axis=1)


def draw_query(key, part):
    layout_dimensions = (N_CTX, 2, BLOCK_TOKENS, HQ * HEAD_SIZE)
    value_rows = jnp.clip(jax.random.normal(jax.random.fold_in(key, 21), layout_dimensions, jnp.float32), -6.0, 6.0)
    return value_rows.astype(jnp.bfloat16)


def draw_key(key, part):
    layout_dimensions = (N_CTX, 2, BLOCK_TOKENS, KEY_VALUE_HEADS * HEAD_SIZE)
    value_rows = jnp.clip(jax.random.normal(jax.random.fold_in(key, 22), layout_dimensions, jnp.float32), -6.0, 6.0)
    return value_rows.astype(jnp.bfloat16)


def draw_doc_start(key, part):
    total = TOKENS
    pieces = 2 * total // BLOCK_TOKENS + 2
    lengths = jax.random.randint(jax.random.fold_in(key, 5), (pieces,), BLOCK_TOKENS // 2, 3 * WIN, dtype=jnp.int32)
    ends = jnp.cumsum(lengths)
    starts = ends - lengths
    positions = jnp.arange(total, dtype=jnp.int32)
    owner = jnp.sum((starts[None, :] <= positions[:, None]).astype(jnp.int32), axis=1) - 1
    first = starts[owner]
    first = jnp.where(positions == total - 1, total - 1, first).astype(jnp.int32)
    return to_storage(first.reshape(2 * N_CTX, BLOCK_TOKENS))


def block_scale(stream_key, extent, cuts, low, high):
    level = 1.0
    for position, shards_of in cuts:
        steps = jax.random.uniform(jax.random.fold_in(jax.random.fold_in(stream_key, 6), position), (shards_of,), jnp.float32, low / len(cuts), high / len(cuts))
        level = level * jnp.repeat(jnp.exp(steps), extent[position] // shards_of).reshape((-1,) + (1,) * (len(extent) - 1 - position))
    return level


def bell_draw(rng, extent, scale, reach, cuts=(), kind=jnp.bfloat16):
    loudness = block_scale(rng, extent, cuts, -0.22, 0.18) if cuts else 1.0
    drawn = jax.random.normal(rng, extent, jnp.float32) * scale * loudness
    return jnp.minimum(jnp.maximum(drawn, -reach), reach).astype(kind)


def setup_inputs(seed: int = 0, part: int = 0) -> dict:
    keys = jax.random.split(jax.random.key(seed), 7)
    part_splits = jax.random.split(jax.random.fold_in(keys[6], part), 7)
    query = draw_query(jax.random.fold_in(jax.random.fold_in(keys[6], part), 71), part)
    key = draw_key(jax.random.fold_in(jax.random.fold_in(keys[6], part), 71), part)
    value = bell_draw(part_splits[2], (N_CTX, 2, BLOCK_TOKENS, KEY_VALUE_HEADS * HEAD_SIZE), 1.0, 6.0, ((0, 8),))
    out_grad = bell_draw(part_splits[3], (N_CTX, 2, BLOCK_TOKENS, HQ * HEAD_SIZE), 1.0, 6.0, ((0, 8),))
    attn_out = bell_draw(part_splits[4], (N_CTX, 2, BLOCK_TOKENS, HQ * HEAD_SIZE), 0.3, 4.0, ((0, 8),))
    doc_start = draw_doc_start(jax.random.fold_in(jax.random.fold_in(keys[6], part), 71), part)
    return dict(query=query, key=key, value=value, out_grad=out_grad, attn_out=attn_out, doc_start=doc_start)


def reference(query, key, value, out_grad, attn_out, doc_start):
    block_length = BLOCK_TOKENS
    window_width = KEY_VALUE_HEADS * HEAD_SIZE
    scale = HEAD_SIZE ** -0.5
    total_length = (STEPS + 1) * block_length
    window = STEPS * block_length

    def in_order(array):
        return jnp.concatenate([array[:, 0], array[::-1, 1]], axis=0)

    def to_store(array):
        half_count = array.shape[0] // 2
        return jnp.stack([array[:half_count], array[half_count:][::-1]], axis=1)

    query_sequence = in_order(query)
    gradient_sequence = in_order(out_grad)
    output_sequence = in_order(attn_out)
    start_seq = in_order(doc_start)
    kv_seq = jnp.concatenate([in_order(key), in_order(value)], axis=-1)
    padding = jnp.zeros((STEPS, block_length, 2 * window_width), kv_seq.dtype)
    kv_padded = jnp.concatenate([padding, kv_seq], axis=0)
    grad_store = jnp.zeros(((2 * N_CTX + STEPS) * block_length, 2 * window_width), jnp.float32)
    offsets = jnp.arange(block_length, dtype=jnp.int32)
    key_offsets = jnp.arange(total_length, dtype=jnp.int32)

    def one_block(carry, index_value):
        query_matrix = query_sequence[index_value].astype(jnp.float32).reshape(block_length, KEY_VALUE_HEADS, QUERY_PER_KV, HEAD_SIZE)
        gradient_list = gradient_sequence[index_value].astype(jnp.float32).reshape(block_length, KEY_VALUE_HEADS, QUERY_PER_KV, HEAD_SIZE)
        output_rows = output_sequence[index_value].astype(jnp.float32).reshape(block_length, KEY_VALUE_HEADS, QUERY_PER_KV, HEAD_SIZE)
        starts = start_seq[index_value]
        window_key_value = lax.dynamic_slice_in_dim(kv_padded, index_value, STEPS + 1, 0).reshape(total_length, 2 * window_width).astype(jnp.float32)
        key_rows = window_key_value[:, :window_width].reshape(total_length, KEY_VALUE_HEADS, HEAD_SIZE)
        value_rows = window_key_value[:, window_width:].reshape(total_length, KEY_VALUE_HEADS, HEAD_SIZE)
        q_pos = index_value * block_length + offsets
        k_pos = (index_value - STEPS) * block_length + key_offsets
        visible = (k_pos[None, :] <= q_pos[:, None]) & (q_pos[:, None] - k_pos[None, :] < window) & (k_pos[None, :] >= starts[:, None])
        scores = jnp.einsum("qkgd,pkd->kgqp", query_matrix, key_rows) * scale
        scores = jnp.where(visible[None, None], scores, -jnp.inf)
        row_max = jnp.max(scores, axis=-1, keepdims=True)
        log_norm = row_max + jnp.log(jnp.sum(jnp.exp(scores - row_max), axis=-1, keepdims=True))
        probs = jnp.exp(scores - log_norm)
        probs_low = lax.optimization_barrier(probs.astype(jnp.bfloat16)).astype(jnp.float32)
        delta = jnp.transpose(jnp.sum(gradient_list * output_rows, axis=-1), (1, 2, 0))
        dprobs = jnp.einsum("qkgd,pkd->kgqp", gradient_list, value_rows)
        dscores = lax.optimization_barrier((probs * (dprobs - delta[..., None])).astype(jnp.bfloat16)).astype(jnp.float32)
        q_part = (jnp.einsum("kgqp,pkd->qkgd", dscores, key_rows) * scale).astype(jnp.bfloat16)
        k_part = jnp.einsum("kgqp,qkgd->pkd", dscores, query_matrix) * scale
        v_part = jnp.einsum("kgqp,qkgd->pkd", probs_low, gradient_list)
        adding = jnp.concatenate([k_part.reshape(total_length, window_width), v_part.reshape(total_length, window_width)], axis=-1)
        begin = (index_value * block_length).astype(jnp.int32)
        current = lax.dynamic_slice_in_dim(carry, begin, total_length, 0)
        carry = lax.dynamic_update_slice_in_dim(carry, current + adding, begin, 0)
        return carry, q_part.reshape(block_length, HQ * HEAD_SIZE)

    grad_store, q_blocks = lax.scan(one_block, grad_store, jnp.arange(2 * N_CTX, dtype=jnp.int32))
    kv_grads = grad_store[STEPS * block_length:].reshape(2 * N_CTX, block_length, 2 * window_width)
    q_grad = to_store(q_blocks)
    k_grad = to_store(kv_grads[..., :window_width]).astype(jnp.bfloat16)
    v_grad = to_store(kv_grads[..., window_width:]).astype(jnp.bfloat16)
    return q_grad, k_grad, v_grad
```

```python
import functools

import jax
import jax.numpy as jnp
from jax import lax
from jax.experimental import pallas as pl
from jax.experimental.pallas import tpu as pltpu
from jax.sharding import PartitionSpec as P

HEAD_SIZE = 128
STEPS = 4
LOG2E = 1.4426950408889634
CONTRACT_LAST = (((1,), (1,)), ((), ()))
CONTRACT_ROWS = (((1,), (0,)), ((), ()))


def dot(a, b, dims=CONTRACT_ROWS):
    return lax.dot_general(a, b, dims, preferred_element_type=jnp.float32)


def stack_heads(rows, first, count):
    return jnp.concatenate(
        [rows[:, (first + a) * HEAD_SIZE : (first + a + 1) * HEAD_SIZE] for a in range(count)],
        axis=0,
    )


def attend(q, do, o, keys, values, low, high, group, scale):
    window = keys.shape[0]
    scores = dot(keys, q, CONTRACT_LAST) * (scale * LOG2E)
    row = lax.broadcasted_iota(jnp.int32, scores.shape, 0)
    scores = jnp.where((row >= low) & (row <= high), scores, -jnp.inf)
    top = jnp.max(scores, axis=0, keepdims=True)
    weights = jnp.exp2(scores - top)
    probs = weights * (1.0 / jnp.sum(weights, axis=0, keepdims=True))
    terms = do.astype(jnp.float32) * o.astype(jnp.float32)
    coarse = terms.astype(jnp.bfloat16)
    fine = (terms - coarse.astype(jnp.float32)).astype(jnp.bfloat16)
    ones = jnp.ones((8, 2 * HEAD_SIZE), jnp.bfloat16)
    delta = dot(ones, jnp.concatenate([coarse, fine], axis=1), CONTRACT_LAST)[:1]
    dprobs = dot(values, do, CONTRACT_LAST)
    dscores = (probs * (dprobs - delta)).astype(jnp.bfloat16)
    v_part = dot(probs.astype(jnp.bfloat16), do)
    k_part = dot(dscores, q) * scale
    q_grad_t = dot(keys.T, dscores) * scale
    return q_grad_t.astype(jnp.bfloat16), k_part, v_part


def kernel(
    block_ref, place_ref, q_ref, do_ref, o_ref, starts_ref, stored_ref,
    dq_ref, dkv_ref, window_ref, sems,
):
    units, tokens, width = q_ref.shape
    heads = width // HEAD_SIZE
    kv_width = stored_ref.shape[-1] // 2
    kv_heads = kv_width // HEAD_SIZE
    group = heads // kv_heads
    scale = HEAD_SIZE ** (-0.5)

    def copy(unit, step):
        place = place_ref[unit * (STEPS + 1) + step]
        return pltpu.make_async_copy(
            stored_ref.at[place],
            window_ref.at[unit, pl.ds(step * tokens, tokens)],
            sems.at[unit, step],
        )

    for unit in range(units):
        for step in range(STEPS + 1):
            copy(unit, step).start()
    dkv_ref[...] = jnp.zeros_like(dkv_ref)
    for unit in range(units):
        for step in range(STEPS + 1):
            copy(unit, step).wait()
        offset = lax.broadcasted_iota(jnp.int32, (1, tokens), 1)
        begin = (block_ref[unit] - STEPS) * tokens
        low = jnp.maximum(offset + 1, starts_ref[unit : unit + 1, :] - begin)
        high = offset + STEPS * tokens
        low = jnp.concatenate([low] * group, axis=1)
        high = jnp.concatenate([high] * group, axis=1)
        for g in range(kv_heads):
            keys = window_ref[unit, :, g * HEAD_SIZE : (g + 1) * HEAD_SIZE]
            values = window_ref[unit, :, kv_width + g * HEAD_SIZE : kv_width + (g + 1) * HEAD_SIZE]
            q = stack_heads(q_ref[unit], g * group, group)
            do = stack_heads(do_ref[unit], g * group, group)
            o = stack_heads(o_ref[unit], g * group, group)
            dq_t, k_part, v_part = attend(q, do, o, keys, values, low, high, group, scale)
            dq = dq_t.T
            for a in range(group):
                dq_ref[unit, :, (g * group + a) * HEAD_SIZE : (g * group + a + 1) * HEAD_SIZE] = (
                    dq[a * tokens : (a + 1) * tokens]
                )
            for step in range(STEPS + 1):
                place = place_ref[unit * (STEPS + 1) + step]
                rows = slice(step * tokens, (step + 1) * tokens)
                for part, at in ((k_part, g * HEAD_SIZE), (v_part, kv_width + g * HEAD_SIZE)):
                    held = dkv_ref[place, :, at : at + HEAD_SIZE].astype(jnp.float32)
                    dkv_ref[place, :, at : at + HEAD_SIZE] = (held + part[rows]).astype(jnp.bfloat16)


def window_backward(blocks, places, query, out_grad, attn_out, starts, stored):
    units, tokens, width = query.shape
    vmem = pl.BlockSpec(memory_space=pltpu.VMEM)
    smem = pl.BlockSpec(memory_space=pltpu.SMEM)
    return pl.pallas_call(
        kernel,
        out_shape=(
            jax.ShapeDtypeStruct((units, tokens, width), jnp.bfloat16),
            jax.ShapeDtypeStruct(stored.shape, jnp.bfloat16),
        ),
        in_specs=[smem, smem, vmem, vmem, vmem, vmem, pl.BlockSpec(memory_space=pl.ANY)],
        out_specs=(vmem, vmem),
        scratch_shapes=[
            pltpu.VMEM((units, (STEPS + 1) * tokens, stored.shape[-1]), jnp.bfloat16),
            pltpu.SemaphoreType.DMA((units, STEPS + 1)),
        ],
        compiler_params=pltpu.CompilerParams(vmem_limit_bytes=48 * 2**20),
        name="window_backward",
    )(blocks, places, query, out_grad, attn_out, starts, stored)


def neighbours(low, high, count):
    forward = [(i, i + 1) for i in range(count - 1)]
    backward = [(target, source) for source, target in forward]
    return lax.ppermute(low, "ctx", forward), lax.ppermute(high, "ctx", backward)


def shards(query, key, value, out_grad, attn_out, doc_start):
    count = lax.axis_size("ctx")
    index = lax.axis_index("ctx")
    blocks = jnp.stack([index, 2 * count - 1 - index]).astype(jnp.int32)
    pair = jnp.concatenate([key[0], value[0]], axis=-1)
    gathers = count <= 2 * STEPS
    is_last = index == count - 1
    if gathers:
        reach = blocks[:, None] - STEPS + jnp.arange(STEPS + 1, dtype=jnp.int32)
        reach = jnp.maximum(reach, 0)
        places = jnp.where(reach < count, 2 * reach, 2 * (2 * count - 1 - reach) + 1).reshape(-1)
        stored = lax.all_gather(pair, "ctx", axis=0, tiled=True)
    else:
        places = jnp.arange(2 * (STEPS + 1), dtype=jnp.int32)
        steps = [pair]
        for _ in range(STEPS):
            low, high = neighbours(steps[-1][0], steps[-1][1], count)
            steps.append(jnp.stack([low, jnp.where(is_last, steps[-1][0], high)]))
        stored = jnp.stack(steps[::-1], axis=1).reshape((-1,) + pair.shape[1:])
    dq, parts = window_backward(
        blocks, places, query[0], out_grad[0], attn_out[0], doc_start[0], stored
    )
    if gathers:
        total = lax.psum_scatter(parts, "ctx", scatter_dimension=0, tiled=True)
    else:
        parts = parts.reshape((2, STEPS + 1) + pair.shape[1:])
        total = parts[:, 0]
        for step in range(1, STEPS + 1):
            high, low = neighbours(total[1], total[0], count)
            total = jnp.stack([jnp.where(is_last, total[1], low), high])
            total = (total.astype(jnp.float32) + parts[:, step]).astype(jnp.bfloat16)
    half = pair.shape[-1] // 2
    return dq[None], total[None, ..., :half], total[None, ..., half:]


def solution(mesh):
    placed = (P("ctx", "dp", None, None),) * 5 + (P("ctx", "dp", None),)
    return jax.shard_map(
        shards,
        mesh=mesh,
        in_specs=placed,
        out_specs=(P("ctx", "dp", None, None),) * 3,
        check_vma=False,
    )
```

```python
import jax
import jax.numpy as jnp
from jax import lax
from jax.experimental import pallas as pl
from jax.experimental.pallas import tpu as pltpu
from jax.sharding import PartitionSpec as P

HEAD_SIZE = 128
STEPS = 4
LOG2E = 1.4426950408889634
CODE = 128
CODE_ROWS = 16
CONTRACT_LAST = (((1,), (1,)), ((), ()))
CONTRACT_ROWS = (((1,), (0,)), ((), ()))
VMEM = pl.BlockSpec(memory_space=pltpu.VMEM)
SMEM = pl.BlockSpec(memory_space=pltpu.SMEM)
ANY = pl.BlockSpec(memory_space=pl.ANY)
PARAMS = pltpu.CompilerParams(vmem_limit_bytes=48 * 2**20)


def dot(a, b, dims=CONTRACT_ROWS):
    return lax.dot_general(a, b, dims, preferred_element_type=jnp.float32)


def stack_heads(ref, first, count):
    return jnp.concatenate(
        [ref[:, (first + a) * HEAD_SIZE : (first + a + 1) * HEAD_SIZE] for a in range(count)],
        axis=0,
    )


def attend(q, do, o, keys, values, low, high, scale):
    scores = dot(keys, q, CONTRACT_LAST) * (scale * LOG2E)
    row = lax.broadcasted_iota(jnp.int32, scores.shape, 0)
    scores = jnp.where((row >= low) & (row <= high), scores, -jnp.inf)
    top = jnp.max(scores, axis=0, keepdims=True)
    weights = jnp.exp2(scores - top)
    probs = weights * (1.0 / jnp.sum(weights, axis=0, keepdims=True))
    terms = do.astype(jnp.float32) * o.astype(jnp.float32)
    coarse = terms.astype(jnp.bfloat16)
    fine = (terms - coarse.astype(jnp.float32)).astype(jnp.bfloat16)
    ones = jnp.ones((8, 2 * HEAD_SIZE), jnp.bfloat16)
    delta = dot(ones, jnp.concatenate([coarse, fine], axis=1), CONTRACT_LAST)[:1]
    dprobs = dot(values, do, CONTRACT_LAST)
    dscores = (probs * (dprobs - delta)).astype(jnp.bfloat16)
    v_part = dot(probs.astype(jnp.bfloat16), do)
    k_part = dot(dscores, q) * scale
    q_grad_t = dot(keys.T, dscores) * scale
    return q_grad_t.astype(jnp.bfloat16), k_part, v_part


def pack_pair_kernel(core_ref, starts_ref, key_ref, value_ref, keep_ref, send_ref, sems):
    core = core_ref[0]
    tokens, width = key_ref.shape[1:]
    copies = []
    for n, (slot, target) in enumerate(((core, keep_ref), (1 - core, send_ref))):
        for m, source in enumerate((key_ref, value_ref)):
            copies.append(
                pltpu.make_async_copy(
                    source.at[slot],
                    target.at[pl.ds(0, tokens), pl.ds(m * width, width)],
                    sems.at[n, m],
                )
            )
    for copy in copies:
        copy.start()
    starts = jnp.where(core == 0, starts_ref[1:2, :], starts_ref[0:1, :])
    coarse = starts // CODE
    coded = jnp.concatenate(
        [coarse, starts - coarse * CODE, jnp.zeros((CODE_ROWS - 2, tokens), jnp.int32)], axis=0
    ).astype(jnp.float32)
    padded = jnp.concatenate(
        [coded, jnp.zeros((CODE_ROWS, 2 * width - tokens), jnp.float32)], axis=1
    )
    send_ref[tokens:, :] = padded.astype(jnp.bfloat16)
    for copy in copies:
        copy.wait()


def pack_rows_kernel(core_ref, q_ref, do_ref, o_ref, send_ref, sems):
    slot = 1 - core_ref[0]
    copies = [
        pltpu.make_async_copy(source.at[slot], send_ref.at[n], sems.at[n])
        for n, source in enumerate((q_ref, do_ref, o_ref))
    ]
    for copy in copies:
        copy.start()
    for copy in copies:
        copy.wait()


def main_kernel(
    place_ref, starts_ref, q_ref, do_ref, o_ref, rows_ref, coded_ref, far_ref, near_ref, own_ref,
    dq_ref, dq_send_ref, far_part_ref, near_part_ref, own_part_ref,
    held_ref, dq_held_ref, window_ref, part_ref, sems, out_sem,
):
    core, begin = place_ref[0], place_ref[1]
    _, tokens, width = q_ref.shape
    heads = width // HEAD_SIZE
    kv_width = own_ref.shape[-1] // 2
    kv_heads = kv_width // HEAD_SIZE
    group = heads // kv_heads
    scale = HEAD_SIZE ** (-0.5)
    reach = (STEPS + 1) * tokens

    copies = []
    for n, source in enumerate((q_ref, do_ref, o_ref)):
        copies.append(
            pltpu.make_async_copy(source.at[core], held_ref.at[n, 0], sems.at[n, 0])
        )
        copies.append(
            pltpu.make_async_copy(rows_ref.at[n], held_ref.at[n, 1], sems.at[n, 1])
        )
    for copy in copies:
        copy.start()
    pair = 2 * tokens
    for n, source in enumerate((far_ref, near_ref, own_ref)):
        window_ref[n * pair : (n + 1) * pair, :] = source[...]
    part_ref[...] = jnp.zeros_like(part_ref)
    coded = coded_ref[tokens : tokens + CODE_ROWS, :tokens].astype(jnp.float32)
    own_starts = jnp.where(core == 0, starts_ref[0:1, :], starts_ref[1:2, :])
    sent_starts = (coded[0:1] * CODE + coded[1:2]).astype(jnp.int32)
    offset = lax.broadcasted_iota(jnp.int32, (1, tokens), 1)
    for copy in copies:
        copy.wait()
    for unit, starts in enumerate((own_starts, sent_starts)):
        first = unit * tokens
        low = jnp.maximum(offset + 1, starts - (begin + (unit - STEPS) * tokens))
        high = offset + STEPS * tokens
        low = jnp.concatenate([low] * group, axis=1)
        high = jnp.concatenate([high] * group, axis=1)
        for g in range(kv_heads):
            at = (g * HEAD_SIZE, kv_width + g * HEAD_SIZE)
            keys = window_ref[first : first + reach, at[0] : at[0] + HEAD_SIZE]
            values = window_ref[first : first + reach, at[1] : at[1] + HEAD_SIZE]
            q = stack_heads(held_ref.at[0, unit], g * group, group)
            do = stack_heads(held_ref.at[1, unit], g * group, group)
            o = stack_heads(held_ref.at[2, unit], g * group, group)
            dq_t, k_part, v_part = attend(q, do, o, keys, values, low, high, scale)
            dq = dq_t.T
            for a in range(group):
                column = (g * group + a) * HEAD_SIZE
                dq_held_ref[unit, :, column : column + HEAD_SIZE] = (
                    dq[a * tokens : (a + 1) * tokens]
                )
            for part, column in ((k_part, at[0]), (v_part, at[1])):
                part_ref[first : first + reach, column : column + HEAD_SIZE] += part
    stores = [
        pltpu.make_async_copy(dq_held_ref.at[0], dq_ref.at[core], out_sem.at[0]),
        pltpu.make_async_copy(dq_held_ref.at[1], dq_send_ref, out_sem.at[1]),
    ]
    for store in stores:
        store.start()
    far_part_ref[...] = part_ref[:pair, :].astype(jnp.bfloat16)
    near_part_ref[...] = part_ref[pair : 2 * pair, :].astype(jnp.bfloat16)
    own_part_ref[...] = part_ref[2 * pair :, :]
    for store in stores:
        store.wait()


def fill_kernel(core_ref, rows_ref, held_ref, out_ref, sem):
    copy = pltpu.make_async_copy(rows_ref, out_ref.at[1 - core_ref[0]], sem)
    copy.start()
    copy.wait()


def shards(query, key, value, out_grad, attn_out, doc_start):
    count = lax.axis_size("ctx")
    index = lax.axis_index("ctx")
    _, slots, tokens, width = query.shape
    kv_width = key.shape[-1]
    pair_width = 2 * kv_width
    pair = 2 * tokens
    core = (index % 2).astype(jnp.int32)
    stage = jnp.where(core == 0, index // 2, count - 1 - index // 2).astype(jnp.int32)
    core = core[None]
    place = jnp.stack([core[0], stage * pair])
    holder = [2 * s if 2 * s < count else 2 * count - 1 - 2 * s for s in range(count)]
    swap = [(i, i ^ 1) for i in range(count)]

    def shift(x, by):
        moves = [
            (holder[s], holder[s + by]) for s in range(count) if 0 <= s + by < count
        ]
        return lax.ppermute(x, "ctx", moves)

    bf16 = jnp.bfloat16
    keep, send = pl.pallas_call(
        pack_pair_kernel,
        out_shape=(
            jax.ShapeDtypeStruct((tokens, pair_width), bf16),
            jax.ShapeDtypeStruct((tokens + CODE_ROWS, pair_width), bf16),
        ),
        in_specs=[SMEM, VMEM, ANY, ANY],
        out_specs=(VMEM, VMEM),
        scratch_shapes=[pltpu.SemaphoreType.DMA((2, 2))],
        name="pack_pair",
    )(core, doc_start[0], key[0], value[0])
    coded = lax.ppermute(send, "ctx", swap)
    own = jnp.concatenate([keep, coded[:tokens]], axis=0)
    own, late_core = lax.optimization_barrier((own, core))
    near = shift(own, 1)
    far = shift(own, 2)
    rows_send = pl.pallas_call(
        pack_rows_kernel,
        out_shape=jax.ShapeDtypeStruct((3, tokens, width), bf16),
        in_specs=[SMEM, ANY, ANY, ANY],
        out_specs=ANY,
        scratch_shapes=[pltpu.SemaphoreType.DMA((3,))],
        name="pack_rows",
    )(late_core, query[0], out_grad[0], attn_out[0])
    rows = lax.ppermute(rows_send, "ctx", swap)
    dq, dq_send, far_part, near_part, own_part = pl.pallas_call(
        main_kernel,
        out_shape=(
            jax.ShapeDtypeStruct((slots, tokens, width), bf16),
            jax.ShapeDtypeStruct((tokens, width), bf16),
            jax.ShapeDtypeStruct((pair, pair_width), bf16),
            jax.ShapeDtypeStruct((pair, pair_width), bf16),
            jax.ShapeDtypeStruct((pair, pair_width), jnp.float32),
        ),
        in_specs=[SMEM, VMEM, ANY, ANY, ANY, ANY, VMEM, VMEM, VMEM, VMEM],
        out_specs=(ANY, ANY, VMEM, VMEM, VMEM),
        scratch_shapes=[
            pltpu.VMEM((3, slots, tokens, width), bf16),
            pltpu.VMEM((slots, tokens, width), bf16),
            pltpu.VMEM((3 * pair, pair_width), bf16),
            pltpu.VMEM((3 * pair, pair_width), jnp.float32),
            pltpu.SemaphoreType.DMA((3, 2)),
            pltpu.SemaphoreType.DMA((2,)),
        ],
        compiler_params=PARAMS,
        name="window_backward",
    )(
        place, doc_start[0], query[0], out_grad[0], attn_out[0], rows, coded, far, near, own
    )
    from_far = shift(far_part, -2)
    from_near = shift(near_part, -1)
    dq_rows = lax.ppermute(dq_send, "ctx", swap)
    dq = pl.pallas_call(
        fill_kernel,
        out_shape=jax.ShapeDtypeStruct(dq.shape, bf16),
        in_specs=[SMEM, ANY, ANY],
        out_specs=ANY,
        scratch_shapes=[pltpu.SemaphoreType.DMA],
        input_output_aliases={2: 0},
        name="fill_rows",
    )(core, dq_rows, dq)
    total = own_part + from_near.astype(jnp.float32) + from_far.astype(jnp.float32)
    total = total.astype(bf16)
    kept = total[:tokens]
    given = lax.ppermute(total[tokens:], "ctx", swap)
    both = jnp.where(core == 0, jnp.stack([kept, given]), jnp.stack([given, kept]))
    return dq[None], both[None, ..., :kv_width], both[None, ..., kv_width:]


def solution(mesh):
    placed = (P("ctx", "dp", None, None),) * 5 + (P("ctx", "dp", None),)
    return jax.shard_map(
        shards,
        mesh=mesh,
        in_specs=placed,
        out_specs=(P("ctx", "dp", None, None),) * 3,
        check_vma=False,
    )
```

```python
import jax
import jax.numpy as jnp
from jax import lax
from jax.experimental import pallas as pl
from jax.experimental.pallas import tpu as pltpu
from jax.sharding import PartitionSpec as P

HEAD_SIZE = 128
STEPS = 4
LOG2E = 1.4426950408889634
CODE = 128
CODE_ROWS = 16
CONTRACT_LAST = (((1,), (1,)), ((), ()))
CONTRACT_ROWS = (((1,), (0,)), ((), ()))
VMEM = pl.BlockSpec(memory_space=pltpu.VMEM)
SMEM = pl.BlockSpec(memory_space=pltpu.SMEM)
ANY = pl.BlockSpec(memory_space=pl.ANY)
PARAMS = pltpu.CompilerParams(vmem_limit_bytes=48 * 2**20)


def dot(a, b, dims=CONTRACT_ROWS):
    return lax.dot_general(a, b, dims, preferred_element_type=jnp.float32)


def stack_heads(ref, first, count):
    return jnp.concatenate(
        [ref[:, (first + a) * HEAD_SIZE : (first + a + 1) * HEAD_SIZE] for a in range(count)],
        axis=0,
    )


def attend(q, do, o, keys, values, low, high, scale):
    scores = dot(keys, q, CONTRACT_LAST) * (scale * LOG2E)
    row = lax.broadcasted_iota(jnp.int32, scores.shape, 0)
    scores = jnp.where((row >= low) & (row <= high), scores, -jnp.inf)
    top = jnp.max(scores, axis=0, keepdims=True)
    weights = jnp.exp2(scores - top)
    probs = weights * (1.0 / jnp.sum(weights, axis=0, keepdims=True))
    terms = do.astype(jnp.float32) * o.astype(jnp.float32)
    coarse = terms.astype(jnp.bfloat16)
    fine = (terms - coarse.astype(jnp.float32)).astype(jnp.bfloat16)
    ones = jnp.ones((8, 2 * HEAD_SIZE), jnp.bfloat16)
    delta = dot(ones, jnp.concatenate([coarse, fine], axis=1), CONTRACT_LAST)[:1]
    dprobs = dot(values, do, CONTRACT_LAST)
    dscores = (probs * (dprobs - delta)).astype(jnp.bfloat16)
    return probs.astype(jnp.bfloat16), dscores


def pack_pair_kernel(
    core_ref, starts_ref, key_ref, value_ref, keep_ref, send_ref, held_ref, sems
):
    copies = [
        pltpu.make_async_copy(source, held_ref.at[n], sems.at[n])
        for n, source in enumerate((key_ref, value_ref))
    ]
    for copy in copies:
        copy.start()
    even = core_ref[0] == 0
    tokens, width = key_ref.shape[1:]
    starts = jnp.where(even, starts_ref[1:2, :], starts_ref[0:1, :])
    coarse = starts // CODE
    coded = jnp.concatenate(
        [coarse, starts - coarse * CODE, jnp.zeros((CODE_ROWS - 2, tokens), jnp.int32)], axis=0
    ).astype(jnp.float32)
    padded = jnp.concatenate(
        [coded, jnp.zeros((CODE_ROWS, 2 * width - tokens), jnp.float32)], axis=1
    )
    send_ref[tokens:, :] = padded.astype(jnp.bfloat16)
    for copy in copies:
        copy.wait()
    core = core_ref[0]
    for n in range(2):
        keep_ref[:, n * width : (n + 1) * width] = held_ref[n, core]
        send_ref[:tokens, n * width : (n + 1) * width] = held_ref[n, 1 - core]


def pack_rows_kernel(core_ref, q_ref, do_ref, o_ref, after_ref, send_ref, sems):
    slot = 1 - core_ref[0]
    copies = [
        pltpu.make_async_copy(source.at[slot], send_ref.at[n], sems.at[n])
        for n, source in enumerate((q_ref, do_ref, o_ref))
    ]
    for copy in copies:
        copy.start()
    for copy in copies:
        copy.wait()


def unit_sizes(rows_ref, pair_ref):
    heads = rows_ref.shape[-1] // HEAD_SIZE
    kv_width = pair_ref.shape[-1] // 2
    kv_heads = kv_width // HEAD_SIZE
    return kv_heads, kv_width, heads // kv_heads


def scores_kernel(
    place_ref, starts_ref, q_ref, do_ref, o_ref, rows_ref, coded_ref, far_ref, near_ref, own_ref,
    far_part_ref, near_part_ref, probs_ref, dscores_ref, window_ref, part_ref,
):
    core, begin = place_ref[0], place_ref[1]
    tokens = q_ref.shape[1]
    kv_heads, kv_width, group = unit_sizes(q_ref, own_ref)
    scale = HEAD_SIZE ** (-0.5)
    reach = (STEPS + 1) * tokens
    pair = 2 * tokens
    for n, source in enumerate((far_ref, near_ref, own_ref)):
        window_ref[n * pair : (n + 1) * pair, :] = source[...]
    coded = coded_ref[tokens : tokens + CODE_ROWS, :tokens].astype(jnp.float32)
    own_starts = jnp.where(core == 0, starts_ref[0:1, :], starts_ref[1:2, :])
    sent_starts = (coded[0:1] * CODE + coded[1:2]).astype(jnp.int32)
    offset = lax.broadcasted_iota(jnp.int32, (1, tokens), 1)
    for unit, starts in enumerate((own_starts, sent_starts)):
        first = unit * tokens
        low = jnp.maximum(offset + 1, starts - (begin + (unit - STEPS) * tokens))
        high = offset + STEPS * tokens
        low = jnp.concatenate([low] * group, axis=1)
        high = jnp.concatenate([high] * group, axis=1)
        sources = [r.at[core] for r in (q_ref, do_ref, o_ref)]
        if unit == 1:
            sources = [rows_ref.at[n] for n in range(3)]
        for g in range(kv_heads):
            at = (g * HEAD_SIZE, kv_width + g * HEAD_SIZE)
            keys = window_ref[first : first + reach, at[0] : at[0] + HEAD_SIZE]
            values = window_ref[first : first + reach, at[1] : at[1] + HEAD_SIZE]
            q, do, o = (stack_heads(r, g * group, group) for r in sources)
            probs, dscores = attend(q, do, o, keys, values, low, high, scale)
            probs_ref[unit, g] = probs
            dscores_ref[unit, g] = dscores
            before = 2 * pair - first
            for part, column in (
                (dot(dscores[:before], q) * scale, at[0]),
                (dot(probs[:before], do), at[1]),
            ):
                columns = slice(column, column + HEAD_SIZE)
                if unit == 0:
                    part_ref[:before, columns] = part
                else:
                    part_ref[first : 2 * pair, columns] += part
    far_part_ref[...] = part_ref[:pair, :].astype(jnp.bfloat16)
    near_part_ref[...] = part_ref[pair:, :].astype(jnp.bfloat16)


def rest_kernel(
    place_ref, q_ref, do_ref, rows_ref, far_ref, near_ref, own_ref, probs_ref, dscores_ref,
    dq_ref, dq_send_ref, own_part_ref, window_ref, held_ref, sem,
):
    core = place_ref[0]
    tokens = q_ref.shape[1]
    kv_heads, kv_width, group = unit_sizes(q_ref, own_ref)
    scale = HEAD_SIZE ** (-0.5)
    reach = (STEPS + 1) * tokens
    pair = 2 * tokens
    for n, source in enumerate((far_ref, near_ref, own_ref)):
        window_ref[n * pair : (n + 1) * pair, :] = source[:, :kv_width]
    store = pltpu.make_async_copy(held_ref, dq_ref.at[core], sem)
    for unit, target in ((1, dq_send_ref), (0, held_ref)):
        first = unit * tokens
        before = 2 * pair - first
        sources = (q_ref.at[core], do_ref.at[core])
        if unit == 1:
            sources = (rows_ref.at[0], rows_ref.at[1])
        for g in range(kv_heads):
            keys = window_ref[first : first + reach, g * HEAD_SIZE : (g + 1) * HEAD_SIZE]
            dq_t = dot(keys.T, dscores_ref[unit, g]) * scale
            dq = dq_t.astype(jnp.bfloat16).T
            for a in range(group):
                column = (g * group + a) * HEAD_SIZE
                target[:, column : column + HEAD_SIZE] = dq[a * tokens : (a + 1) * tokens]
            q, do = (stack_heads(r, g * group, group) for r in sources)
            at = (g * HEAD_SIZE, kv_width + g * HEAD_SIZE)
            for part, column in (
                (dot(dscores_ref[unit, g, before:, :], q) * scale, at[0]),
                (dot(probs_ref[unit, g, before:, :], do), at[1]),
            ):
                columns = slice(column, column + HEAD_SIZE)
                if unit == 1:
                    own_part_ref[:, columns] = part
                else:
                    own_part_ref[:tokens, columns] += part
    store.start()
    store.wait()


def fill_kernel(core_ref, rows_ref, held_ref, out_ref, sem):
    copy = pltpu.make_async_copy(rows_ref, out_ref.at[1 - core_ref[0]], sem)
    copy.start()
    copy.wait()


def shards(query, key, value, out_grad, attn_out, doc_start):
    count = lax.axis_size("ctx")
    index = lax.axis_index("ctx")
    _, slots, tokens, width = query.shape
    kv_width = key.shape[-1]
    pair_width = 2 * kv_width
    pair = 2 * tokens
    core = (index % 2).astype(jnp.int32)
    stage = jnp.where(core == 0, index // 2, count - 1 - index // 2).astype(jnp.int32)
    core = core[None]
    place = jnp.stack([core[0], stage * pair])
    holder = [2 * s if 2 * s < count else 2 * count - 1 - 2 * s for s in range(count)]
    swap = [(i, i ^ 1) for i in range(count)]

    def shift(x, by):
        moves = [
            (holder[s], holder[s + by]) for s in range(count) if 0 <= s + by < count
        ]
        return lax.ppermute(x, "ctx", moves)

    bf16 = jnp.bfloat16
    keep, send = pl.pallas_call(
        pack_pair_kernel,
        out_shape=(
            jax.ShapeDtypeStruct((tokens, pair_width), bf16),
            jax.ShapeDtypeStruct((tokens + CODE_ROWS, pair_width), bf16),
        ),
        in_specs=[SMEM, VMEM, ANY, ANY],
        out_specs=(VMEM, VMEM),
        scratch_shapes=[
            pltpu.VMEM((2, slots, tokens, kv_width), bf16),
            pltpu.SemaphoreType.DMA((2,)),
        ],
        name="pack_pair",
    )(core, doc_start[0], key[0], value[0])
    coded = lax.ppermute(send, "ctx", swap)
    rows_send = pl.pallas_call(
        pack_rows_kernel,
        out_shape=jax.ShapeDtypeStruct((3, tokens, width), bf16),
        in_specs=[SMEM, ANY, ANY, ANY, ANY],
        out_specs=VMEM,
        scratch_shapes=[pltpu.SemaphoreType.DMA((3,))],
        name="pack_rows",
    )(core, query[0], out_grad[0], attn_out[0], keep)
    coded, rows_send = lax.optimization_barrier((coded, rows_send))
    own = jnp.concatenate([keep, coded[:tokens]], axis=0)
    far = shift(own, 2)
    near = shift(own, 1)
    rows = lax.ppermute(rows_send, "ctx", swap)
    reach = (STEPS + 1) * tokens
    kv_heads = kv_width // HEAD_SIZE
    lanes = tokens * (width // kv_width)
    held = jax.ShapeDtypeStruct((slots, kv_heads, reach, lanes), bf16)
    far_part, near_part, probs, dscores = pl.pallas_call(
        scores_kernel,
        out_shape=(
            jax.ShapeDtypeStruct((pair, pair_width), bf16),
            jax.ShapeDtypeStruct((pair, pair_width), bf16),
            held,
            held,
        ),
        in_specs=[SMEM] + [VMEM] * 9,
        out_specs=(VMEM,) * 4,
        scratch_shapes=[
            pltpu.VMEM((3 * pair, pair_width), bf16),
            pltpu.VMEM((2 * pair, pair_width), jnp.float32),
        ],
        compiler_params=PARAMS,
        name="scores",
    )(
        place, doc_start[0], query[0], out_grad[0], attn_out[0], rows, coded, far, near, own
    )
    from_far = shift(far_part, -2)
    from_near = shift(near_part, -1)
    dq, dq_send, own_part = pl.pallas_call(
        rest_kernel,
        out_shape=(
            jax.ShapeDtypeStruct((slots, tokens, width), bf16),
            jax.ShapeDtypeStruct((tokens, width), bf16),
            jax.ShapeDtypeStruct((pair, pair_width), jnp.float32),
        ),
        in_specs=[SMEM] + [VMEM] * 8,
        out_specs=(ANY, VMEM, VMEM),
        scratch_shapes=[
            pltpu.VMEM((3 * pair, kv_width), bf16),
            pltpu.VMEM((tokens, width), bf16),
            pltpu.SemaphoreType.DMA,
        ],
        compiler_params=PARAMS,
        name="rest",
    )(place, query[0], out_grad[0], rows, far, near, own, probs, dscores)
    dq_rows = lax.ppermute(dq_send, "ctx", swap)
    dq = pl.pallas_call(
        fill_kernel,
        out_shape=jax.ShapeDtypeStruct(dq.shape, bf16),
        in_specs=[SMEM, VMEM, ANY],
        out_specs=ANY,
        scratch_shapes=[pltpu.SemaphoreType.DMA],
        input_output_aliases={2: 0},
        name="fill_rows",
    )(core, dq_rows, dq)
    total = own_part + from_near.astype(jnp.float32) + from_far.astype(jnp.float32)
    total = total.astype(bf16)
    kept = total[:tokens]
    given = lax.ppermute(total[tokens:], "ctx", swap)
    both = jnp.where(core == 0, jnp.stack([kept, given]), jnp.stack([given, kept]))
    return dq[None], both[None, ..., :kv_width], both[None, ..., kv_width:]


def solution(mesh):
    placed = (P("ctx", "dp", None, None),) * 5 + (P("ctx", "dp", None),)
    return jax.shard_map(
        shards,
        mesh=mesh,
        in_specs=placed,
        out_specs=(P("ctx", "dp", None, None),) * 3,
        check_vma=False,
    )
```

```python
import jax
import jax.numpy as jnp
from jax import lax
from jax.experimental import pallas as pl
from jax.experimental.pallas import tpu as pltpu
from jax.sharding import PartitionSpec as P

HEAD_SIZE = 128
STEPS = 4
LOG2E = 1.4426950408889634
CONTRACT_LAST = (((1,), (1,)), ((), ()))
CONTRACT_ROWS = (((1,), (0,)), ((), ()))
VMEM = pl.BlockSpec(memory_space=pltpu.VMEM)
SMEM = pl.BlockSpec(memory_space=pltpu.SMEM)
HBM = pl.BlockSpec(memory_space=pltpu.HBM)
PARAMS = pltpu.CompilerParams(vmem_limit_bytes=24 * 2**20)
SMALL = pltpu.CompilerParams(vmem_limit_bytes=4 * 2**20)


def dot(a, b, dims=CONTRACT_ROWS):
    return lax.dot_general(a, b, dims, preferred_element_type=jnp.float32)


def stack_heads(ref, first, count):
    return jnp.concatenate(
        [ref[:, (first + a) * HEAD_SIZE : (first + a + 1) * HEAD_SIZE] for a in range(count)],
        axis=0,
    )


def attend(q, do, o, keys, values, low, high, scale):
    scores = dot(keys, q, CONTRACT_LAST) * (scale * LOG2E)
    row = lax.broadcasted_iota(jnp.int32, scores.shape, 0)
    scores = jnp.where((row >= low) & (row <= high), scores, -jnp.inf)
    top = jnp.max(scores, axis=0, keepdims=True)
    weights = jnp.exp2(scores - top)
    probs = weights * (1.0 / jnp.sum(weights, axis=0, keepdims=True))
    terms = do.astype(jnp.float32) * o.astype(jnp.float32)
    coarse = terms.astype(jnp.bfloat16)
    fine = (terms - coarse.astype(jnp.float32)).astype(jnp.bfloat16)
    ones = jnp.ones((8, 2 * HEAD_SIZE), jnp.bfloat16)
    delta = dot(ones, jnp.concatenate([coarse, fine], axis=1), CONTRACT_LAST)[:1]
    dprobs = dot(values, do, CONTRACT_LAST)
    dscores = (probs * (dprobs - delta)).astype(jnp.bfloat16)
    return probs.astype(jnp.bfloat16), dscores


def unit_sizes(rows_ref, pair_ref):
    heads = rows_ref.shape[-1] // HEAD_SIZE
    kv_width = pair_ref.shape[-1] // 2
    kv_heads = kv_width // HEAD_SIZE
    return kv_heads, kv_width, heads // kv_heads


def scores_kernel(
    place_ref, starts_ref, q_ref, do_ref, o_ref, starts_in_ref, q_in_ref, do_in_ref, o_in_ref,
    far_ref, near_ref, own_ref, far_part_ref, near_part_ref, probs_ref, dscores_ref,
    window_ref, part_ref,
):
    core, begin = place_ref[0], place_ref[1]
    tokens = q_ref.shape[1]
    kv_heads, kv_width, group = unit_sizes(q_ref, own_ref)
    scale = HEAD_SIZE ** (-0.5)
    reach = (STEPS + 1) * tokens
    pair = 2 * tokens
    for n, source in enumerate((far_ref, near_ref, own_ref)):
        window_ref[n * pair : (n + 1) * pair, :] = source[...]
    offset = lax.broadcasted_iota(jnp.int32, (1, tokens), 1)
    sides = ((starts_ref, q_ref, do_ref, o_ref), (starts_in_ref, q_in_ref, do_in_ref, o_in_ref))
    for unit, (starts_side, *sources) in enumerate(sides):
        starts = jnp.where(core == 0, starts_side[0:1, :], starts_side[1:2, :])
        first = unit * tokens
        low = jnp.maximum(offset + 1, starts - (begin + (unit - STEPS) * tokens))
        high = offset + STEPS * tokens
        low = jnp.concatenate([low] * group, axis=1)
        high = jnp.concatenate([high] * group, axis=1)
        for g in range(kv_heads):
            at = (g * HEAD_SIZE, kv_width + g * HEAD_SIZE)
            keys = window_ref[first : first + reach, at[0] : at[0] + HEAD_SIZE]
            values = window_ref[first : first + reach, at[1] : at[1] + HEAD_SIZE]
            q, do, o = (stack_heads(r.at[core], g * group, group) for r in sources)
            probs, dscores = attend(q, do, o, keys, values, low, high, scale)
            probs_ref[unit, g] = probs
            dscores_ref[unit, g] = dscores
            before = 2 * pair - first
            for part, column in (
                (dot(dscores[:before], q) * scale, at[0]),
                (dot(probs[:before], do), at[1]),
            ):
                columns = slice(column, column + HEAD_SIZE)
                if unit == 0:
                    part_ref[:before, columns] = part
                else:
                    part_ref[first : 2 * pair, columns] += part
    far_part_ref[...] = part_ref[:pair, :].astype(jnp.bfloat16)
    near_part_ref[...] = part_ref[pair:, :].astype(jnp.bfloat16)


def rest_kernel(
    place_ref, q_ref, do_ref, q_in_ref, do_in_ref, far_ref, near_ref, own_ref, probs_ref,
    dscores_ref, dq_ref, dq_send_ref, own_part_ref, window_ref, held_ref, sem,
):
    core = place_ref[0]
    tokens = q_ref.shape[1]
    kv_heads, kv_width, group = unit_sizes(q_ref, own_ref)
    scale = HEAD_SIZE ** (-0.5)
    reach = (STEPS + 1) * tokens
    pair = 2 * tokens
    for n, source in enumerate((far_ref, near_ref, own_ref)):
        window_ref[n * pair : (n + 1) * pair, :] = source[:, :kv_width]
    store = pltpu.make_async_copy(held_ref, dq_ref.at[core], sem)
    sides = ((1, dq_send_ref, q_in_ref, do_in_ref), (0, held_ref, q_ref, do_ref))
    for unit, target, *sources in sides:
        first = unit * tokens
        before = 2 * pair - first
        for g in range(kv_heads):
            keys = window_ref[first : first + reach, g * HEAD_SIZE : (g + 1) * HEAD_SIZE]
            dq_t = dot(keys.T, dscores_ref[unit, g]) * scale
            dq = dq_t.astype(jnp.bfloat16).T
            for a in range(group):
                column = (g * group + a) * HEAD_SIZE
                target[:, column : column + HEAD_SIZE] = dq[a * tokens : (a + 1) * tokens]
            if unit == 0 and g == kv_heads - 1:
                store.start()
            q, do = (stack_heads(r.at[core], g * group, group) for r in sources)
            at = (g * HEAD_SIZE, kv_width + g * HEAD_SIZE)
            for part, column in (
                (dot(dscores_ref[unit, g, before:, :], q) * scale, at[0]),
                (dot(probs_ref[unit, g, before:, :], do), at[1]),
            ):
                columns = slice(column, column + HEAD_SIZE)
                if unit == 1:
                    own_part_ref[:, columns] = part
                else:
                    own_part_ref[:tokens, columns] += part
    store.wait()


def store_kernel(
    core_ref, rows_ref, kept_ref, given_ref, held_ref, dq_ref, key_ref, value_ref, sems
):
    core = core_ref[0]
    width = key_ref.shape[-1]
    copies = [pltpu.make_async_copy(rows_ref, dq_ref.at[1 - core], sems.at[0, 0])]
    for n, (source, slot) in enumerate(((kept_ref, core), (given_ref, 1 - core))):
        for m, target in enumerate((key_ref, value_ref)):
            copies.append(
                pltpu.make_async_copy(
                    source.at[:, pl.ds(m * width, width)], target.at[slot], sems.at[n + 1, m]
                )
            )
    for copy in copies:
        copy.start()
    for copy in copies:
        copy.wait()


def shards(query, key, value, out_grad, attn_out, doc_start):
    count = lax.axis_size("ctx")
    index = lax.axis_index("ctx")
    _, slots, tokens, width = query.shape
    kv_width = key.shape[-1]
    pair_width = 2 * kv_width
    pair = 2 * tokens
    core = (index % 2).astype(jnp.int32)
    stage = jnp.where(core == 0, index // 2, count - 1 - index // 2).astype(jnp.int32)
    core = core[None]
    place = jnp.stack([core[0], stage * pair])
    holder = [2 * s if 2 * s < count else 2 * count - 1 - 2 * s for s in range(count)]
    swap = [(i, i ^ 1) for i in range(count)]

    def shift(x, by):
        moves = [
            (holder[s], holder[s + by]) for s in range(count) if 0 <= s + by < count
        ]
        return lax.ppermute(x, "ctx", moves)

    bf16 = jnp.bfloat16
    def swapped(x):
        return lax.ppermute(x, "ctx", swap)

    def mine(x):
        return jnp.where(core == 0, x[0], x[1])

    starts_in, key_in, value_in = (swapped(x[0]) for x in (doc_start, key, value))
    sides = ((key[0], value[0]), (key_in, value_in))
    own = jnp.concatenate(
        [jnp.concatenate([mine(x) for x in side], axis=-1) for side in sides], axis=0
    )
    own, starts_in, *late = lax.optimization_barrier(
        (own, starts_in, query, out_grad, attn_out)
    )
    sent = [starts_in] + [swapped(x[0]) for x in late]
    far = shift(own, 2)
    near = shift(own, 1)
    reach = (STEPS + 1) * tokens
    kv_heads = kv_width // HEAD_SIZE
    lanes = tokens * (width // kv_width)
    products = 2 * slots * tokens * reach * width

    def work(flops, moved):
        return pl.CostEstimate(flops=flops, bytes_accessed=moved, transcendentals=0)

    held = jax.ShapeDtypeStruct((slots, kv_heads, reach, lanes), bf16)
    far_part, near_part, probs, dscores = pl.pallas_call(
        scores_kernel,
        out_shape=(
            jax.ShapeDtypeStruct((pair, pair_width), bf16),
            jax.ShapeDtypeStruct((pair, pair_width), bf16),
            held,
            held,
        ),
        in_specs=[SMEM] + [VMEM] * 11,
        out_specs=(VMEM,) * 4,
        scratch_shapes=[
            pltpu.VMEM((3 * pair, pair_width), bf16),
            pltpu.VMEM((2 * pair, pair_width), jnp.float32),
        ],
        compiler_params=PARAMS,
        cost_estimate=work(3 * products, 12 * 2**20),
        name="scores",
    )(place, doc_start[0], query[0], out_grad[0], attn_out[0], *sent, far, near, own)
    from_far = shift(far_part, -2)
    from_near = shift(near_part, -1)
    dq, dq_send, own_part = pl.pallas_call(
        rest_kernel,
        out_shape=(
            jax.ShapeDtypeStruct((slots, tokens, width), bf16),
            jax.ShapeDtypeStruct((tokens, width), bf16),
            jax.ShapeDtypeStruct((pair, pair_width), jnp.float32),
        ),
        in_specs=[SMEM] + [VMEM] * 9,
        out_specs=(HBM, VMEM, VMEM),
        scratch_shapes=[
            pltpu.VMEM((3 * pair, kv_width), bf16),
            pltpu.VMEM((tokens, width), bf16),
            pltpu.SemaphoreType.DMA,
        ],
        compiler_params=PARAMS,
        cost_estimate=work(3 * products // 2, 8 * 2**20),
        name="rest",
    )(place, query[0], out_grad[0], *sent[1:3], far, near, own, probs, dscores)
    from_near, from_far, dq_send = lax.optimization_barrier((from_near, from_far, dq_send))
    dq_rows = swapped(dq_send)
    total = own_part + from_near.astype(jnp.float32) + from_far.astype(jnp.float32)
    total = total.astype(bf16)
    kept = total[:tokens]
    given = swapped(total[tokens:])
    dq, dk, dv = pl.pallas_call(
        store_kernel,
        out_shape=(
            jax.ShapeDtypeStruct(dq.shape, bf16),
            jax.ShapeDtypeStruct((slots, tokens, kv_width), bf16),
            jax.ShapeDtypeStruct((slots, tokens, kv_width), bf16),
        ),
        in_specs=[SMEM, VMEM, VMEM, VMEM, HBM],
        out_specs=(HBM,) * 3,
        scratch_shapes=[pltpu.SemaphoreType.DMA((3, 2))],
        input_output_aliases={4: 0},
        compiler_params=SMALL,
        name="store",
    )(core, dq_rows, kept, given, dq)
    return dq[None], dk[None], dv[None]


def solution(mesh):
    placed = (P("ctx", "dp", None, None),) * 5 + (P("ctx", "dp", None),)
    return jax.shard_map(
        shards,
        mesh=mesh,
        in_specs=placed,
        out_specs=(P("ctx", "dp", None, None),) * 3,
        check_vma=False,
    )
```

```python
import jax
import jax.numpy as jnp
from jax import lax
from jax.experimental import pallas as pl
from jax.experimental.pallas import tpu as pltpu
from jax.sharding import PartitionSpec as P

HEAD_SIZE = 128
STEPS = 4
LOG2E = 1.4426950408889634
CONTRACT_LAST = (((1,), (1,)), ((), ()))
CONTRACT_ROWS = (((1,), (0,)), ((), ()))
VMEM = pl.BlockSpec(memory_space=pltpu.VMEM)
SMEM = pl.BlockSpec(memory_space=pltpu.SMEM)
HBM = pl.BlockSpec(memory_space=pltpu.HBM)
PARAMS = pltpu.CompilerParams(vmem_limit_bytes=24 * 2**20)
SMALL = pltpu.CompilerParams(vmem_limit_bytes=4 * 2**20)


def dot(a, b, dims=CONTRACT_ROWS):
    return lax.dot_general(a, b, dims, preferred_element_type=jnp.float32)


def stack_heads(ref, first, count):
    return jnp.concatenate(
        [ref[:, (first + a) * HEAD_SIZE : (first + a + 1) * HEAD_SIZE] for a in range(count)],
        axis=0,
    )


def attend(q, do, o, keys, values, low, high, scale):
    scores = dot(keys, q, CONTRACT_LAST) * (scale * LOG2E)
    row = lax.broadcasted_iota(jnp.int32, scores.shape, 0)
    scores = jnp.where((row >= low) & (row <= high), scores, -jnp.inf)
    top = jnp.max(scores, axis=0, keepdims=True)
    weights = jnp.exp2(scores - top)
    probs = weights * (1.0 / jnp.sum(weights, axis=0, keepdims=True))
    terms = do.astype(jnp.float32) * o.astype(jnp.float32)
    coarse = terms.astype(jnp.bfloat16)
    fine = (terms - coarse.astype(jnp.float32)).astype(jnp.bfloat16)
    ones = jnp.ones((8, 2 * HEAD_SIZE), jnp.bfloat16)
    delta = dot(ones, jnp.concatenate([coarse, fine], axis=1), CONTRACT_LAST)[:1]
    dprobs = dot(values, do, CONTRACT_LAST)
    dscores = (probs * (dprobs - delta)).astype(jnp.bfloat16)
    return probs.astype(jnp.bfloat16), dscores


def unit_sizes(rows_ref, pair_ref):
    heads = rows_ref.shape[-1] // HEAD_SIZE
    kv_width = pair_ref.shape[-1] // 2
    kv_heads = kv_width // HEAD_SIZE
    return kv_heads, kv_width, heads // kv_heads


def scores_kernel(
    place_ref, starts_ref, q_ref, do_ref, o_ref, q_in_ref, do_in_ref, o_in_ref,
    far_ref, near_ref, own_ref, far_part_ref, near_part_ref, probs_ref, dscores_ref,
    window_ref, part_ref,
):
    core, begin = place_ref[0], place_ref[1]
    tokens = q_ref.shape[1]
    kv_heads, kv_width, group = unit_sizes(q_ref, own_ref)
    scale = HEAD_SIZE ** (-0.5)
    reach = (STEPS + 1) * tokens
    pair = 2 * tokens
    for n, source in enumerate((far_ref, near_ref, own_ref)):
        window_ref[n * pair : (n + 1) * pair, :] = source[...]
    offset = lax.broadcasted_iota(jnp.int32, (1, tokens), 1)
    sides = ((q_ref, do_ref, o_ref), (q_in_ref, do_in_ref, o_in_ref))
    for unit, sources in enumerate(sides):
        starts_side = starts_ref[2 * unit : 2 * unit + 2, :]
        starts = jnp.where(core == 0, starts_side[0:1, :], starts_side[1:2, :])
        first = unit * tokens
        low = jnp.maximum(offset + 1, starts - (begin + (unit - STEPS) * tokens))
        high = offset + STEPS * tokens
        low = jnp.concatenate([low] * group, axis=1)
        high = jnp.concatenate([high] * group, axis=1)
        for g in range(kv_heads):
            at = (g * HEAD_SIZE, kv_width + g * HEAD_SIZE)
            keys = window_ref[first : first + reach, at[0] : at[0] + HEAD_SIZE]
            values = window_ref[first : first + reach, at[1] : at[1] + HEAD_SIZE]
            q, do, o = (stack_heads(r.at[core], g * group, group) for r in sources)
            probs, dscores = attend(q, do, o, keys, values, low, high, scale)
            probs_ref[unit, g] = probs
            dscores_ref[unit, g] = dscores
            before = 2 * pair - first
            for part, column in (
                (dot(dscores[:before], q) * scale, at[0]),
                (dot(probs[:before], do), at[1]),
            ):
                columns = slice(column, column + HEAD_SIZE)
                if unit == 0:
                    part_ref[:before, columns] = part
                else:
                    part_ref[first : 2 * pair, columns] += part
    far_part_ref[...] = part_ref[:pair, :].astype(jnp.bfloat16)
    near_part_ref[...] = part_ref[pair:, :].astype(jnp.bfloat16)


def rest_kernel(
    place_ref, q_ref, do_ref, q_in_ref, do_in_ref, far_ref, near_ref, own_ref, probs_ref,
    dscores_ref, dq_ref, dq_send_ref, own_part_ref, window_ref, held_ref, sem,
):
    core = place_ref[0]
    tokens = q_ref.shape[1]
    kv_heads, kv_width, group = unit_sizes(q_ref, own_ref)
    scale = HEAD_SIZE ** (-0.5)
    reach = (STEPS + 1) * tokens
    pair = 2 * tokens
    for n, source in enumerate((far_ref, near_ref, own_ref)):
        window_ref[n * pair : (n + 1) * pair, :] = source[:, :kv_width]
    store = pltpu.make_async_copy(held_ref, dq_ref.at[core], sem)
    sides = ((1, dq_send_ref, q_in_ref, do_in_ref), (0, held_ref, q_ref, do_ref))
    for unit, target, *sources in sides:
        first = unit * tokens
        before = 2 * pair - first
        for g in range(kv_heads):
            keys = window_ref[first : first + reach, g * HEAD_SIZE : (g + 1) * HEAD_SIZE]
            dq_t = dot(keys.T, dscores_ref[unit, g]) * scale
            dq = dq_t.astype(jnp.bfloat16).T
            for a in range(group):
                column = (g * group + a) * HEAD_SIZE
                target[:, column : column + HEAD_SIZE] = dq[a * tokens : (a + 1) * tokens]
            if unit == 0 and g == kv_heads - 1:
                store.start()
            q, do = (stack_heads(r.at[core], g * group, group) for r in sources)
            at = (g * HEAD_SIZE, kv_width + g * HEAD_SIZE)
            for part, column in (
                (dot(dscores_ref[unit, g, before:, :], q) * scale, at[0]),
                (dot(probs_ref[unit, g, before:, :], do), at[1]),
            ):
                columns = slice(column, column + HEAD_SIZE)
                if unit == 1:
                    own_part_ref[:, columns] = part
                else:
                    own_part_ref[:tokens, columns] += part
    store.wait()


def store_kernel(
    core_ref, rows_ref, kept_ref, given_ref, held_ref, dq_ref, key_ref, value_ref, sems
):
    core = core_ref[0]
    width = key_ref.shape[-1]
    copies = [pltpu.make_async_copy(rows_ref, dq_ref.at[1 - core], sems.at[0, 0])]
    for n, (source, slot) in enumerate(((kept_ref, core), (given_ref, 1 - core))):
        for m, target in enumerate((key_ref, value_ref)):
            copies.append(
                pltpu.make_async_copy(
                    source.at[:, pl.ds(m * width, width)], target.at[slot], sems.at[n + 1, m]
                )
            )
    for copy in copies:
        copy.start()
    for copy in copies:
        copy.wait()


def shards(query, key, value, out_grad, attn_out, doc_start):
    count = lax.axis_size("ctx")
    index = lax.axis_index("ctx")
    _, slots, tokens, width = query.shape
    kv_width = key.shape[-1]
    pair_width = 2 * kv_width
    pair = 2 * tokens
    core = (index % 2).astype(jnp.int32)
    stage = jnp.where(core == 0, index // 2, count - 1 - index // 2).astype(jnp.int32)
    core = core[None]
    place = jnp.stack([core[0], stage * pair])
    holder = [2 * s if 2 * s < count else 2 * count - 1 - 2 * s for s in range(count)]
    swap = [(i, i ^ 1) for i in range(count)]

    def shift(x, by):
        moves = [
            (holder[s], holder[s + by]) for s in range(count) if 0 <= s + by < count
        ]
        return lax.ppermute(x, "ctx", moves)

    bf16 = jnp.bfloat16
    def swapped(x):
        return lax.ppermute(x, "ctx", swap)

    def mine(x):
        return jnp.where(core == 0, x[0], x[1])

    starts_in, key_in, value_in = (swapped(x[0]) for x in (doc_start, key, value))
    sides = ((key[0], value[0]), (key_in, value_in))
    own = jnp.concatenate(
        [jnp.concatenate([mine(x) for x in side], axis=-1) for side in sides], axis=0
    )
    starts = jnp.concatenate([doc_start[0], starts_in], axis=0)
    own, starts, *late = lax.optimization_barrier(
        (own, starts, query[0], out_grad[0], attn_out[0])
    )
    sent = [swapped(x) for x in late]
    far = shift(own, 2)
    near = shift(own, 1)
    reach = (STEPS + 1) * tokens
    kv_heads = kv_width // HEAD_SIZE
    lanes = tokens * (width // kv_width)
    products = 2 * slots * tokens * reach * width

    def work(flops, moved):
        return pl.CostEstimate(flops=flops, bytes_accessed=moved, transcendentals=0)

    held = jax.ShapeDtypeStruct((slots, kv_heads, reach, lanes), bf16)
    far_part, near_part, probs, dscores = pl.pallas_call(
        scores_kernel,
        out_shape=(
            jax.ShapeDtypeStruct((pair, pair_width), bf16),
            jax.ShapeDtypeStruct((pair, pair_width), bf16),
            held,
            held,
        ),
        in_specs=[SMEM] + [VMEM] * 10,
        out_specs=(VMEM,) * 4,
        scratch_shapes=[
            pltpu.VMEM((3 * pair, pair_width), bf16),
            pltpu.VMEM((2 * pair, pair_width), jnp.float32),
        ],
        compiler_params=PARAMS,
        cost_estimate=work(3 * products, 12 * 2**20),
        name="scores",
    )(place, starts, *late, *sent, far, near, own)
    from_far = shift(far_part, -2)
    from_near = shift(near_part, -1)
    dq, dq_send, own_part = pl.pallas_call(
        rest_kernel,
        out_shape=(
            jax.ShapeDtypeStruct((slots, tokens, width), bf16),
            jax.ShapeDtypeStruct((tokens, width), bf16),
            jax.ShapeDtypeStruct((pair, pair_width), jnp.float32),
        ),
        in_specs=[SMEM] + [VMEM] * 9,
        out_specs=(HBM, VMEM, VMEM),
        scratch_shapes=[
            pltpu.VMEM((3 * pair, kv_width), bf16),
            pltpu.VMEM((tokens, width), bf16),
            pltpu.SemaphoreType.DMA,
        ],
        compiler_params=PARAMS,
        cost_estimate=work(3 * products // 2, 8 * 2**20),
        name="rest",
    )(place, *late[:2], *sent[:2], far, near, own, probs, dscores)
    from_near, from_far, dq_send = lax.optimization_barrier((from_near, from_far, dq_send))
    dq_rows = swapped(dq_send)
    total = own_part + from_near.astype(jnp.float32) + from_far.astype(jnp.float32)
    total = total.astype(bf16)
    kept = total[:tokens]
    given = swapped(total[tokens:])
    dq, dk, dv = pl.pallas_call(
        store_kernel,
        out_shape=(
            jax.ShapeDtypeStruct(dq.shape, bf16),
            jax.ShapeDtypeStruct((slots, tokens, kv_width), bf16),
            jax.ShapeDtypeStruct((slots, tokens, kv_width), bf16),
        ),
        in_specs=[SMEM, VMEM, VMEM, VMEM, HBM],
        out_specs=(HBM,) * 3,
        scratch_shapes=[pltpu.SemaphoreType.DMA((3, 2))],
        input_output_aliases={4: 0},
        compiler_params=SMALL,
        name="store",
    )(core, dq_rows, kept, given, dq)
    return dq[None], dk[None], dv[None]


def solution(mesh):
    placed = (P("ctx", "dp", None, None),) * 5 + (P("ctx", "dp", None),)
    return jax.shard_map(
        shards,
        mesh=mesh,
        in_specs=placed,
        out_specs=(P("ctx", "dp", None, None),) * 3,
        check_vma=False,
    )
```

```python
import jax
import jax.numpy as jnp
from jax import lax
from jax.experimental import pallas as pl
from jax.experimental.pallas import tpu as pltpu
from jax.sharding import PartitionSpec as P

HEAD_SIZE = 128
STEPS = 4
LOG2E = 1.4426950408889634
CONTRACT_LAST = (((1,), (1,)), ((), ()))
CONTRACT_ROWS = (((1,), (0,)), ((), ()))
VMEM = pl.BlockSpec(memory_space=pltpu.VMEM)
SMEM = pl.BlockSpec(memory_space=pltpu.SMEM)
HBM = pl.BlockSpec(memory_space=pltpu.HBM)
PARAMS = pltpu.CompilerParams(vmem_limit_bytes=24 * 2**20)
SMALL = pltpu.CompilerParams(vmem_limit_bytes=4 * 2**20)


def dot(a, b, dims=CONTRACT_ROWS):
    return lax.dot_general(a, b, dims, preferred_element_type=jnp.float32)


def stack_heads(ref, first, count):
    return jnp.concatenate(
        [ref[:, (first + a) * HEAD_SIZE : (first + a + 1) * HEAD_SIZE] for a in range(count)],
        axis=0,
    )


def attend(q, do, delta, keys, values, low, high, scale):
    scores = dot(keys, q, CONTRACT_LAST) * (scale * LOG2E)
    row = lax.broadcasted_iota(jnp.int32, scores.shape, 0)
    scores = jnp.where((row >= low) & (row <= high), scores, -jnp.inf)
    top = jnp.max(scores, axis=0, keepdims=True)
    weights = jnp.exp2(scores - top)
    probs = weights * (1.0 / jnp.sum(weights, axis=0, keepdims=True))
    dprobs = dot(values, do, CONTRACT_LAST)
    dscores = (probs * (dprobs - delta)).astype(jnp.bfloat16)
    return probs.astype(jnp.bfloat16), dscores


def rows_kernel(core_ref, q_ref, do_ref, o_ref, q_out_ref, do_out_ref, delta_ref):
    core = core_ref[0]
    group = q_out_ref.shape[1] // q_ref.shape[1]
    ones = jnp.ones((delta_ref.shape[1], 2 * HEAD_SIZE), jnp.bfloat16)
    for g in range(q_out_ref.shape[0]):
        q, do, o = (
            stack_heads(r.at[core], g * group, group) for r in (q_ref, do_ref, o_ref)
        )
        terms = do.astype(jnp.float32) * o.astype(jnp.float32)
        coarse = terms.astype(jnp.bfloat16)
        fine = (terms - coarse.astype(jnp.float32)).astype(jnp.bfloat16)
        delta_ref[g] = dot(ones, jnp.concatenate([coarse, fine], axis=1), CONTRACT_LAST)
        q_out_ref[g] = q
        do_out_ref[g] = do


def scores_kernel(
    place_ref, starts_ref, q_ref, do_ref, delta_ref, q_in_ref, do_in_ref, delta_in_ref,
    far_ref, near_ref, own_ref, far_part_ref, near_part_ref, probs_ref, dscores_ref,
    window_ref, part_ref,
):
    core, begin = place_ref[0], place_ref[1]
    tokens = starts_ref.shape[1]
    kv_heads, lanes = q_ref.shape[:2]
    kv_width = kv_heads * HEAD_SIZE
    group = lanes // tokens
    scale = HEAD_SIZE ** (-0.5)
    reach = (STEPS + 1) * tokens
    pair = 2 * tokens
    for n, source in enumerate((far_ref, near_ref, own_ref)):
        window_ref[n * pair : (n + 1) * pair, :] = source[...]
    offset = lax.broadcasted_iota(jnp.int32, (1, tokens), 1)
    sides = ((q_ref, do_ref, delta_ref), (q_in_ref, do_in_ref, delta_in_ref))
    for unit, (q_side, do_side, delta_side) in enumerate(sides):
        starts_side = starts_ref[2 * unit : 2 * unit + 2, :]
        starts = jnp.where(core == 0, starts_side[0:1, :], starts_side[1:2, :])
        first = unit * tokens
        low = jnp.maximum(offset + 1, starts - (begin + (unit - STEPS) * tokens))
        high = offset + STEPS * tokens
        low = jnp.concatenate([low] * group, axis=1)
        high = jnp.concatenate([high] * group, axis=1)
        for g in range(kv_heads):
            at = (g * HEAD_SIZE, kv_width + g * HEAD_SIZE)
            keys = window_ref[first : first + reach, at[0] : at[0] + HEAD_SIZE]
            values = window_ref[first : first + reach, at[1] : at[1] + HEAD_SIZE]
            q, do = q_side[g], do_side[g]
            probs, dscores = attend(q, do, delta_side[g, :1], keys, values, low, high, scale)
            probs_ref[unit, g] = probs
            dscores_ref[unit, g] = dscores
            before = 2 * pair - first
            for part, column in (
                (dot(dscores[:before], q) * scale, at[0]),
                (dot(probs[:before], do), at[1]),
            ):
                columns = slice(column, column + HEAD_SIZE)
                if unit == 0:
                    part_ref[:before, columns] = part
                else:
                    part_ref[first : 2 * pair, columns] += part
    far_part_ref[...] = part_ref[:pair, :].astype(jnp.bfloat16)
    near_part_ref[...] = part_ref[pair:, :].astype(jnp.bfloat16)


def rest_kernel(
    place_ref, q_ref, do_ref, q_in_ref, do_in_ref, far_ref, near_ref, own_ref, probs_ref,
    dscores_ref, dq_ref, dq_send_ref, own_part_ref, window_ref, held_ref, sem,
):
    core = place_ref[0]
    tokens = dq_send_ref.shape[0]
    kv_heads, lanes = q_ref.shape[:2]
    kv_width = kv_heads * HEAD_SIZE
    group = lanes // tokens
    scale = HEAD_SIZE ** (-0.5)
    reach = (STEPS + 1) * tokens
    pair = 2 * tokens
    for n, source in enumerate((far_ref, near_ref, own_ref)):
        window_ref[n * pair : (n + 1) * pair, :] = source[:, :kv_width]
    store = pltpu.make_async_copy(held_ref, dq_ref.at[core], sem)
    sides = ((1, dq_send_ref, q_in_ref, do_in_ref), (0, held_ref, q_ref, do_ref))
    for unit, target, q_side, do_side in sides:
        first = unit * tokens
        before = 2 * pair - first
        for g in range(kv_heads):
            keys = window_ref[first : first + reach, g * HEAD_SIZE : (g + 1) * HEAD_SIZE]
            dq_t = dot(keys.T, dscores_ref[unit, g]) * scale
            dq = dq_t.astype(jnp.bfloat16).T
            for a in range(group):
                column = (g * group + a) * HEAD_SIZE
                target[:, column : column + HEAD_SIZE] = dq[a * tokens : (a + 1) * tokens]
            if unit == 0 and g == kv_heads - 1:
                store.start()
            at = (g * HEAD_SIZE, kv_width + g * HEAD_SIZE)
            for part, column in (
                (dot(dscores_ref[unit, g, before:, :], q_side[g]) * scale, at[0]),
                (dot(probs_ref[unit, g, before:, :], do_side[g]), at[1]),
            ):
                columns = slice(column, column + HEAD_SIZE)
                if unit == 1:
                    own_part_ref[:, columns] = part
                else:
                    own_part_ref[:tokens, columns] += part
    store.wait()


def store_kernel(
    core_ref, rows_ref, kept_ref, given_ref, held_ref, dq_ref, key_ref, value_ref, sems
):
    core = core_ref[0]
    width = key_ref.shape[-1]
    copies = [pltpu.make_async_copy(rows_ref, dq_ref.at[1 - core], sems.at[0, 0])]
    for n, (source, slot) in enumerate(((kept_ref, core), (given_ref, 1 - core))):
        for m, target in enumerate((key_ref, value_ref)):
            copies.append(
                pltpu.make_async_copy(
                    source.at[:, pl.ds(m * width, width)], target.at[slot], sems.at[n + 1, m]
                )
            )
    for copy in copies:
        copy.start()
    for copy in copies:
        copy.wait()


def shards(query, key, value, out_grad, attn_out, doc_start):
    count = lax.axis_size("ctx")
    index = lax.axis_index("ctx")
    _, slots, tokens, width = query.shape
    kv_width = key.shape[-1]
    pair_width = 2 * kv_width
    pair = 2 * tokens
    core = (index % 2).astype(jnp.int32)
    stage = jnp.where(core == 0, index // 2, count - 1 - index // 2).astype(jnp.int32)
    core = core[None]
    place = jnp.stack([core[0], stage * pair])
    holder = [2 * s if 2 * s < count else 2 * count - 1 - 2 * s for s in range(count)]
    swap = [(i, i ^ 1) for i in range(count)]

    def shift(x, by):
        moves = [
            (holder[s], holder[s + by]) for s in range(count) if 0 <= s + by < count
        ]
        return lax.ppermute(x, "ctx", moves)

    bf16 = jnp.bfloat16
    def work(flops, moved):
        return pl.CostEstimate(flops=flops, bytes_accessed=moved, transcendentals=0)

    def swapped(x):
        return lax.ppermute(x, "ctx", swap)

    def mine(x):
        return jnp.where(core == 0, x[0], x[1])

    starts_in, key_in, value_in = (swapped(x[0]) for x in (doc_start, key, value))
    sides = ((key[0], value[0]), (key_in, value_in))
    own = jnp.concatenate(
        [jnp.concatenate([mine(x) for x in side], axis=-1) for side in sides], axis=0
    )
    starts = jnp.concatenate([doc_start[0], starts_in], axis=0)
    own, starts, *late = lax.optimization_barrier(
        (own, starts, query[0], out_grad[0], attn_out[0])
    )
    kv_heads = kv_width // HEAD_SIZE
    lanes = tokens * (width // kv_width)

    def arranged(sources):
        stacked = jax.ShapeDtypeStruct((kv_heads, lanes, HEAD_SIZE), bf16)
        return pl.pallas_call(
            rows_kernel,
            out_shape=(
                stacked,
                stacked,
                jax.ShapeDtypeStruct((kv_heads, 8, lanes), jnp.float32),
            ),
            in_specs=[SMEM] + [VMEM] * 3,
            out_specs=(VMEM,) * 3,
            compiler_params=SMALL,
            cost_estimate=work(2**20, 4 * 2**20),
            name="rows",
        )(core, *sources)

    sent = [swapped(x) for x in late]
    rows, rows_in = arranged(late), arranged(sent)
    far = shift(own, 2)
    near = shift(own, 1)
    reach = (STEPS + 1) * tokens
    products = 2 * slots * tokens * reach * width

    held = jax.ShapeDtypeStruct((slots, kv_heads, reach, lanes), bf16)
    far_part, near_part, probs, dscores = pl.pallas_call(
        scores_kernel,
        out_shape=(
            jax.ShapeDtypeStruct((pair, pair_width), bf16),
            jax.ShapeDtypeStruct((pair, pair_width), bf16),
            held,
            held,
        ),
        in_specs=[SMEM] + [VMEM] * 10,
        out_specs=(VMEM,) * 4,
        scratch_shapes=[
            pltpu.VMEM((3 * pair, pair_width), bf16),
            pltpu.VMEM((2 * pair, pair_width), jnp.float32),
        ],
        compiler_params=PARAMS,
        cost_estimate=work(3 * products, 12 * 2**20),
        name="scores",
    )(place, starts, *rows, *rows_in, far, near, own)
    from_far = shift(far_part, -2)
    from_near = shift(near_part, -1)
    dq, dq_send, own_part = pl.pallas_call(
        rest_kernel,
        out_shape=(
            jax.ShapeDtypeStruct((slots, tokens, width), bf16),
            jax.ShapeDtypeStruct((tokens, width), bf16),
            jax.ShapeDtypeStruct((pair, pair_width), jnp.float32),
        ),
        in_specs=[SMEM] + [VMEM] * 9,
        out_specs=(HBM, VMEM, VMEM),
        scratch_shapes=[
            pltpu.VMEM((3 * pair, kv_width), bf16),
            pltpu.VMEM((tokens, width), bf16),
            pltpu.SemaphoreType.DMA,
        ],
        compiler_params=PARAMS,
        cost_estimate=work(3 * products // 2, 8 * 2**20),
        name="rest",
    )(place, *rows[:2], *rows_in[:2], far, near, own, probs, dscores)
    from_near, from_far, dq_send = lax.optimization_barrier((from_near, from_far, dq_send))
    dq_rows = swapped(dq_send)
    total = own_part + from_near.astype(jnp.float32) + from_far.astype(jnp.float32)
    total = total.astype(bf16)
    kept = total[:tokens]
    given = swapped(total[tokens:])
    dq, dk, dv = pl.pallas_call(
        store_kernel,
        out_shape=(
            jax.ShapeDtypeStruct(dq.shape, bf16),
            jax.ShapeDtypeStruct((slots, tokens, kv_width), bf16),
            jax.ShapeDtypeStruct((slots, tokens, kv_width), bf16),
        ),
        in_specs=[SMEM, VMEM, VMEM, VMEM, HBM],
        out_specs=(HBM,) * 3,
        scratch_shapes=[pltpu.SemaphoreType.DMA((3, 2))],
        input_output_aliases={4: 0},
        compiler_params=SMALL,
        name="store",
    )(core, dq_rows, kept, given, dq)
    return dq[None], dk[None], dv[None]


def solution(mesh):
    placed = (P("ctx", "dp", None, None),) * 5 + (P("ctx", "dp", None),)
    return jax.shard_map(
        shards,
        mesh=mesh,
        in_specs=placed,
        out_specs=(P("ctx", "dp", None, None),) * 3,
        check_vma=False,
    )
```

```python
import functools

import jax
import jax.numpy as jnp
from jax import lax
from jax.experimental import pallas as pl
from jax.experimental.pallas import tpu as pltpu
from jax.sharding import PartitionSpec as P

HEAD_SIZE = 128
STEPS = 4
LOG2E = 1.4426950408889634
CONTRACT_LAST = (((1,), (1,)), ((), ()))
CONTRACT_ROWS = (((1,), (0,)), ((), ()))
VMEM = pl.BlockSpec(memory_space=pltpu.VMEM)
SMEM = pl.BlockSpec(memory_space=pltpu.SMEM)
HBM = pl.BlockSpec(memory_space=pltpu.HBM)
PARAMS = pltpu.CompilerParams(vmem_limit_bytes=24 * 2**20)
SMALL = pltpu.CompilerParams(vmem_limit_bytes=4 * 2**20)


def dot(a, b, dims=CONTRACT_ROWS):
    return lax.dot_general(a, b, dims, preferred_element_type=jnp.float32)


def stack_heads(ref, first, count):
    return jnp.concatenate(
        [ref[:, (first + a) * HEAD_SIZE : (first + a + 1) * HEAD_SIZE] for a in range(count)],
        axis=0,
    )


def unit_starts(starts_ref, core, unit):
    side = starts_ref[2 * unit : 2 * unit + 2, :]
    return jnp.where(core == 0, side[0:1, :], side[1:2, :])


def rows_kernel(
    unit, place_ref, starts_ref, own_ref, q_ref, do_ref, o_ref,
    q_out_ref, do_out_ref, scores_ref, dprobs_ref, delta_ref,
):
    core, begin = place_ref[0], place_ref[1]
    tokens = q_ref.shape[1]
    kv_heads, reach, lanes = scores_ref.shape
    kv_width = kv_heads * HEAD_SIZE
    group = lanes // tokens
    factor = HEAD_SIZE ** (-0.5) * LOG2E
    ones = jnp.ones((delta_ref.shape[1], 2 * HEAD_SIZE), jnp.bfloat16)
    low = unit_starts(starts_ref, core, unit) - begin
    high = lax.broadcasted_iota(jnp.int32, (1, tokens), 1) + unit * tokens
    row = lax.broadcasted_iota(jnp.int32, (reach, tokens), 0)
    bias = jnp.where((row >= low) & (row <= high), 0.0, -jnp.inf)
    bias = jnp.concatenate([bias] * group, axis=1)
    for g in range(kv_heads):
        q, do, o = (
            stack_heads(r.at[core], g * group, group) for r in (q_ref, do_ref, o_ref)
        )
        keys = own_ref[:reach, g * HEAD_SIZE : (g + 1) * HEAD_SIZE]
        values = own_ref[:reach, kv_width + g * HEAD_SIZE : kv_width + (g + 1) * HEAD_SIZE]
        terms = do.astype(jnp.float32) * o.astype(jnp.float32)
        coarse = terms.astype(jnp.bfloat16)
        fine = (terms - coarse.astype(jnp.float32)).astype(jnp.bfloat16)
        delta = dot(ones, jnp.concatenate([coarse, fine], axis=1), CONTRACT_LAST)
        delta_ref[g] = delta
        scores_ref[g] = dot(keys, q, CONTRACT_LAST) * factor + bias
        dprobs_ref[g] = dot(values, do, CONTRACT_LAST) - delta[:1]
        q_out_ref[g] = q
        do_out_ref[g] = do


def scores_kernel(
    place_ref, starts_ref, q_ref, do_ref, held_ref, delta_ref, q_in_ref, do_in_ref, held_in_ref,
    delta_in_ref, far_ref, near_ref, far_part_ref, near_part_ref, dscores_ref, norm_ref,
    window_ref, part_ref,
):
    core, begin = place_ref[0], place_ref[1]
    tokens = starts_ref.shape[1]
    kv_heads, lanes = q_ref.shape[:2]
    kv_width = kv_heads * HEAD_SIZE
    group = lanes // tokens
    scale = HEAD_SIZE ** (-0.5)
    pair = 2 * tokens
    for n, source in enumerate((far_ref, near_ref)):
        window_ref[n * pair : (n + 1) * pair, :] = source[...]
    offset = lax.broadcasted_iota(jnp.int32, (1, tokens), 1)
    sides = (
        (q_ref, do_ref, held_ref, delta_ref), (q_in_ref, do_in_ref, held_in_ref, delta_in_ref)
    )
    for unit, (q_side, do_side, held_side, delta_side) in enumerate(sides):
        first = unit * tokens
        before = 2 * pair - first
        low = unit_starts(starts_ref, core, unit) - (begin + (unit - STEPS) * tokens)
        low = jnp.maximum(offset + 1, low)
        low = jnp.concatenate([low] * group, axis=1)
        for g in range(kv_heads):
            at = (g * HEAD_SIZE, kv_width + g * HEAD_SIZE)
            keys = window_ref[first:, at[0] : at[0] + HEAD_SIZE]
            values = window_ref[first:, at[1] : at[1] + HEAD_SIZE]
            q, do, held = q_side[g], do_side[g], held_side[g]
            scores = dot(keys, q, CONTRACT_LAST) * (scale * LOG2E)
            row = lax.broadcasted_iota(jnp.int32, scores.shape, 0)
            scores = jnp.where(row >= low, scores, -jnp.inf)
            top = jnp.maximum(
                jnp.max(scores, axis=0, keepdims=True), jnp.max(held, axis=0, keepdims=True)
            )
            weights = jnp.exp2(scores - top)
            total = jnp.sum(weights, axis=0, keepdims=True)
            total += jnp.sum(jnp.exp2(held - top), axis=0, keepdims=True)
            inverse = 1.0 / total
            probs = weights * inverse
            norm_ref[unit, g, 0:1] = top
            norm_ref[unit, g, 1:2] = inverse
            dprobs = dot(values, do, CONTRACT_LAST) - delta_side[g, :1]
            dscores = (probs * dprobs).astype(jnp.bfloat16)
            dscores_ref[unit, g, :before] = dscores
            for part, column in (
                (dot(dscores, q) * scale, at[0]),
                (dot(probs.astype(jnp.bfloat16), do), at[1]),
            ):
                columns = slice(column, column + HEAD_SIZE)
                if unit == 0:
                    part_ref[:, columns] = part
                else:
                    part_ref[first:, columns] += part
    far_part_ref[...] = part_ref[:pair, :].astype(jnp.bfloat16)
    near_part_ref[...] = part_ref[pair:, :].astype(jnp.bfloat16)


def rest_kernel(
    place_ref, q_ref, do_ref, held_ref, dprobs_ref, q_in_ref, do_in_ref, held_in_ref,
    dprobs_in_ref, far_ref, near_ref, own_ref, dscores_ref, norm_ref,
    dq_ref, dq_send_ref, own_part_ref, window_ref, rows_ref, sem,
):
    core = place_ref[0]
    tokens = dq_send_ref.shape[0]
    kv_heads, lanes = q_ref.shape[:2]
    kv_width = kv_heads * HEAD_SIZE
    group = lanes // tokens
    scale = HEAD_SIZE ** (-0.5)
    pair = 2 * tokens
    for n, source in enumerate((far_ref, near_ref)):
        window_ref[n * pair : (n + 1) * pair, :] = source[:, :kv_width]
    store = pltpu.make_async_copy(rows_ref, dq_ref.at[core], sem)
    sides = (
        (1, dq_send_ref, q_in_ref, do_in_ref, held_in_ref, dprobs_in_ref),
        (0, rows_ref, q_ref, do_ref, held_ref, dprobs_ref),
    )
    for unit, target, q_side, do_side, held_side, dprobs_side in sides:
        first = unit * tokens
        before = 2 * pair - first
        reach = held_side.shape[1]
        for g in range(kv_heads):
            at = (g * HEAD_SIZE, kv_width + g * HEAD_SIZE)
            top, inverse = norm_ref[unit, g, 0:1], norm_ref[unit, g, 1:2]
            probs = jnp.exp2(held_side[g] - top) * inverse
            dscores = (probs * dprobs_side[g]).astype(jnp.bfloat16)
            keys = window_ref[first:, at[0] : at[0] + HEAD_SIZE]
            own_keys = own_ref[:reach, at[0] : at[0] + HEAD_SIZE]
            dq_t = dot(keys.T, dscores_ref[unit, g, :before]) + dot(own_keys.T, dscores)
            dq = (dq_t * scale).astype(jnp.bfloat16).T
            for a in range(group):
                column = (g * group + a) * HEAD_SIZE
                target[:, column : column + HEAD_SIZE] = dq[a * tokens : (a + 1) * tokens]
            if unit == 0 and g == kv_heads - 1:
                store.start()
            for part, column in (
                (dot(dscores, q_side[g]) * scale, at[0]),
                (dot(probs.astype(jnp.bfloat16), do_side[g]), at[1]),
            ):
                columns = slice(column, column + HEAD_SIZE)
                if unit == 1:
                    own_part_ref[:, columns] = part
                else:
                    own_part_ref[:reach, columns] += part
    store.wait()


def store_kernel(
    core_ref, rows_ref, kept_ref, given_ref, held_ref, dq_ref, key_ref, value_ref, sems
):
    core = core_ref[0]
    width = key_ref.shape[-1]
    copies = [pltpu.make_async_copy(rows_ref, dq_ref.at[1 - core], sems.at[0, 0])]
    for n, (source, slot) in enumerate(((kept_ref, core), (given_ref, 1 - core))):
        for m, target in enumerate((key_ref, value_ref)):
            copies.append(
                pltpu.make_async_copy(
                    source.at[:, pl.ds(m * width, width)], target.at[slot], sems.at[n + 1, m]
                )
            )
    for copy in copies:
        copy.start()
    for copy in copies:
        copy.wait()


def shards(query, key, value, out_grad, attn_out, doc_start):
    count = lax.axis_size("ctx")
    index = lax.axis_index("ctx")
    _, slots, tokens, width = query.shape
    kv_width = key.shape[-1]
    pair_width = 2 * kv_width
    pair = 2 * tokens
    core = (index % 2).astype(jnp.int32)
    stage = jnp.where(core == 0, index // 2, count - 1 - index // 2).astype(jnp.int32)
    core = core[None]
    place = jnp.stack([core[0], stage * pair])
    holder = [2 * s if 2 * s < count else 2 * count - 1 - 2 * s for s in range(count)]
    swap = [(i, i ^ 1) for i in range(count)]

    def shift(x, by):
        moves = [
            (holder[s], holder[s + by]) for s in range(count) if 0 <= s + by < count
        ]
        return lax.ppermute(x, "ctx", moves)

    bf16 = jnp.bfloat16
    def work(flops, moved):
        return pl.CostEstimate(flops=flops, bytes_accessed=moved, transcendentals=0)

    def swapped(x):
        return lax.ppermute(x, "ctx", swap)

    def mine(x):
        return jnp.where(core == 0, x[0], x[1])

    starts_in, key_in, value_in = (swapped(x[0]) for x in (doc_start, key, value))
    sides = ((key[0], value[0]), (key_in, value_in))
    own = jnp.concatenate(
        [jnp.concatenate([mine(x) for x in side], axis=-1) for side in sides], axis=0
    )
    own, starts_in, starts, *late = lax.optimization_barrier(
        (own, starts_in, doc_start[0], query[0], out_grad[0], attn_out[0])
    )
    starts = jnp.concatenate([starts, starts_in], axis=0)
    kv_heads = kv_width // HEAD_SIZE
    lanes = tokens * (width // kv_width)
    products = 2 * slots * tokens * pair * width

    def arranged(unit, sources):
        stacked = jax.ShapeDtypeStruct((kv_heads, lanes, HEAD_SIZE), bf16)
        square = jax.ShapeDtypeStruct((kv_heads, (unit + 1) * tokens, lanes), jnp.float32)
        q, do, scores, dprobs, delta = pl.pallas_call(
            functools.partial(rows_kernel, unit),
            out_shape=(
                stacked,
                stacked,
                square,
                square,
                jax.ShapeDtypeStruct((kv_heads, 8, lanes), jnp.float32),
            ),
            in_specs=[SMEM] + [VMEM] * 5,
            out_specs=(VMEM,) * 5,
            compiler_params=SMALL,
            cost_estimate=work(products // 2, 4 * 2**20),
            name="rows",
        )(place, starts, own, *sources)
        return (q, do, scores, delta), (q, do, scores, dprobs)

    sent = [swapped(x) for x in late]
    far = shift(own, 2)
    near = shift(own, 1)
    sides = arranged(0, late), arranged(1, sent)
    far_part, near_part, dscores, norm = pl.pallas_call(
        scores_kernel,
        out_shape=(
            jax.ShapeDtypeStruct((pair, pair_width), bf16),
            jax.ShapeDtypeStruct((pair, pair_width), bf16),
            jax.ShapeDtypeStruct((slots, kv_heads, 2 * pair, lanes), bf16),
            jax.ShapeDtypeStruct((slots, kv_heads, 8, lanes), jnp.float32),
        ),
        in_specs=[SMEM] + [VMEM] * 11,
        out_specs=(VMEM,) * 4,
        scratch_shapes=[
            pltpu.VMEM((2 * pair, pair_width), bf16),
            pltpu.VMEM((2 * pair, pair_width), jnp.float32),
        ],
        compiler_params=PARAMS,
        cost_estimate=work(6 * products, 12 * 2**20),
        name="scores",
    )(place, starts, *sides[0][0], *sides[1][0], far, near)
    from_far = shift(far_part, -2)
    from_near = shift(near_part, -1)
    dq, dq_send, own_part = pl.pallas_call(
        rest_kernel,
        out_shape=(
            jax.ShapeDtypeStruct((slots, tokens, width), bf16),
            jax.ShapeDtypeStruct((tokens, width), bf16),
            jax.ShapeDtypeStruct((pair, pair_width), jnp.float32),
        ),
        in_specs=[SMEM] + [VMEM] * 13,
        out_specs=(HBM, VMEM, VMEM),
        scratch_shapes=[
            pltpu.VMEM((2 * pair, kv_width), bf16),
            pltpu.VMEM((tokens, width), bf16),
            pltpu.SemaphoreType.DMA,
        ],
        compiler_params=PARAMS,
        cost_estimate=work(3 * products, 8 * 2**20),
        name="rest",
    )(place, *sides[0][1], *sides[1][1], far, near, own, dscores, norm)
    from_near, from_far, dq_send = lax.optimization_barrier((from_near, from_far, dq_send))
    dq_rows = swapped(dq_send)
    total = own_part + from_near.astype(jnp.float32) + from_far.astype(jnp.float32)
    total = total.astype(bf16)
    kept = total[:tokens]
    given = swapped(total[tokens:])
    dq, dk, dv = pl.pallas_call(
        store_kernel,
        out_shape=(
            jax.ShapeDtypeStruct(dq.shape, bf16),
            jax.ShapeDtypeStruct((slots, tokens, kv_width), bf16),
            jax.ShapeDtypeStruct((slots, tokens, kv_width), bf16),
        ),
        in_specs=[SMEM, VMEM, VMEM, VMEM, HBM],
        out_specs=(HBM,) * 3,
        scratch_shapes=[pltpu.SemaphoreType.DMA((3, 2))],
        input_output_aliases={4: 0},
        compiler_params=SMALL,
        name="store",
    )(core, dq_rows, kept, given, dq)
    return dq[None], dk[None], dv[None]


def solution(mesh):
    placed = (P("ctx", "dp", None, None),) * 5 + (P("ctx", "dp", None),)
    return jax.shard_map(
        shards,
        mesh=mesh,
        in_specs=placed,
        out_specs=(P("ctx", "dp", None, None),) * 3,
        check_vma=False,
    )
```

```python
import functools

import jax
import jax.numpy as jnp
from jax import lax
from jax.experimental import pallas as pl
from jax.experimental.pallas import tpu as pltpu
from jax.sharding import PartitionSpec as P

HEAD_SIZE = 128
STEPS = 4
LOG2E = 1.4426950408889634
CONTRACT_LAST = (((1,), (1,)), ((), ()))
CONTRACT_ROWS = (((1,), (0,)), ((), ()))
VMEM = pl.BlockSpec(memory_space=pltpu.VMEM)
SMEM = pl.BlockSpec(memory_space=pltpu.SMEM)
HBM = pl.BlockSpec(memory_space=pltpu.HBM)
PARAMS = pltpu.CompilerParams(vmem_limit_bytes=24 * 2**20)
SMALL = pltpu.CompilerParams(vmem_limit_bytes=4 * 2**20)


def dot(a, b, dims=CONTRACT_ROWS):
    return lax.dot_general(a, b, dims, preferred_element_type=jnp.float32)


def stack_heads(ref, first, count):
    return jnp.concatenate(
        [ref[:, (first + a) * HEAD_SIZE : (first + a + 1) * HEAD_SIZE] for a in range(count)],
        axis=0,
    )


def unit_starts(starts_ref, core):
    return jnp.where(core == 0, starts_ref[0:1, :], starts_ref[1:2, :])


def rows_kernel(
    unit, place_ref, starts_ref, own_ref, q_ref, do_ref, o_ref,
    q_out_ref, do_out_ref, scores_ref, dprobs_ref, delta_ref,
):
    core, begin = place_ref[0], place_ref[1]
    tokens = q_ref.shape[1]
    kv_heads, reach, lanes = scores_ref.shape
    kv_width = kv_heads * HEAD_SIZE
    group = lanes // tokens
    factor = HEAD_SIZE ** (-0.5) * LOG2E
    ones = jnp.ones((delta_ref.shape[1], 2 * HEAD_SIZE), jnp.bfloat16)
    low = unit_starts(starts_ref, core) - begin
    high = lax.broadcasted_iota(jnp.int32, (1, tokens), 1) + unit * tokens
    row = lax.broadcasted_iota(jnp.int32, (reach, tokens), 0)
    bias = jnp.where((row >= low) & (row <= high), 0.0, -jnp.inf)
    bias = jnp.concatenate([bias] * group, axis=1)
    for g in range(kv_heads):
        q, do, o = (
            stack_heads(r.at[core], g * group, group) for r in (q_ref, do_ref, o_ref)
        )
        keys = own_ref[:reach, g * HEAD_SIZE : (g + 1) * HEAD_SIZE]
        values = own_ref[:reach, kv_width + g * HEAD_SIZE : kv_width + (g + 1) * HEAD_SIZE]
        terms = do.astype(jnp.float32) * o.astype(jnp.float32)
        coarse = terms.astype(jnp.bfloat16)
        fine = (terms - coarse.astype(jnp.float32)).astype(jnp.bfloat16)
        delta = dot(ones, jnp.concatenate([coarse, fine], axis=1), CONTRACT_LAST)
        delta_ref[g] = delta
        scores_ref[g] = dot(keys, q, CONTRACT_LAST) * factor + bias
        dprobs_ref[g] = dot(values, do, CONTRACT_LAST) - delta[:1]
        q_out_ref[g] = q
        do_out_ref[g] = do


def scores_kernel(
    place_ref, starts_ref, q_ref, do_ref, held_ref, delta_ref,
    starts_in_ref, q_in_ref, do_in_ref, held_in_ref, delta_in_ref, far_ref, near_ref,
    far_part_ref, near_part_ref, dscores_ref, norm_ref, window_ref, part_ref,
):
    core, begin = place_ref[0], place_ref[1]
    tokens = starts_ref.shape[1]
    kv_heads, lanes = q_ref.shape[:2]
    kv_width = kv_heads * HEAD_SIZE
    group = lanes // tokens
    scale = HEAD_SIZE ** (-0.5)
    pair = 2 * tokens
    for n, source in enumerate((far_ref, near_ref)):
        window_ref[n * pair : (n + 1) * pair, :] = source[...]
    offset = lax.broadcasted_iota(jnp.int32, (1, tokens), 1)
    sides = (
        (starts_ref, q_ref, do_ref, held_ref, delta_ref),
        (starts_in_ref, q_in_ref, do_in_ref, held_in_ref, delta_in_ref),
    )

    def products(unit, g):
        starts, q_side, do_side, held_side, delta_side = sides[unit]
        first = unit * tokens
        columns = slice(g * HEAD_SIZE, (g + 1) * HEAD_SIZE)
        values = window_ref[first:, kv_width + g * HEAD_SIZE : kv_width + (g + 1) * HEAD_SIZE]
        low = unit_starts(starts, core) - (begin + (unit - STEPS) * tokens)
        low = jnp.concatenate([jnp.maximum(offset + 1, low)] * group, axis=1)
        scores = dot(window_ref[first:, columns], q_side[g], CONTRACT_LAST) * (scale * LOG2E)
        row = lax.broadcasted_iota(jnp.int32, scores.shape, 0)
        scores = jnp.where(row >= low, scores, -jnp.inf)
        return scores, dot(values, do_side[g], CONTRACT_LAST)

    order = [(unit, g) for unit in range(2) for g in range(kv_heads)]
    ahead = products(*order[0])
    for step, (unit, g) in enumerate(order):
        scores, dprobs = ahead
        if step + 1 < len(order):
            ahead = products(*order[step + 1])
        _, q_side, do_side, held_side, delta_side = sides[unit]
        first = unit * tokens
        before = 2 * pair - first
        held = held_side[g]
        top = jnp.maximum(
            jnp.max(scores, axis=0, keepdims=True), jnp.max(held, axis=0, keepdims=True)
        )
        weights = jnp.exp2(scores - top)
        total = jnp.sum(weights, axis=0, keepdims=True)
        total += jnp.sum(jnp.exp2(held - top), axis=0, keepdims=True)
        inverse = 1.0 / total
        probs = weights * inverse
        norm_ref[unit, g, 0:1] = top
        norm_ref[unit, g, 1:2] = inverse
        dscores = (probs * (dprobs - delta_side[g, :1])).astype(jnp.bfloat16)
        dscores_ref[unit, g, :before] = dscores
        for part, column in (
            (dot(dscores, q_side[g]) * scale, g * HEAD_SIZE),
            (dot(probs.astype(jnp.bfloat16), do_side[g]), kv_width + g * HEAD_SIZE),
        ):
            columns = slice(column, column + HEAD_SIZE)
            if unit == 0:
                part_ref[:, columns] = part
            else:
                part_ref[first:, columns] += part
    far_part_ref[...] = part_ref[:pair, :].astype(jnp.bfloat16)
    near_part_ref[...] = part_ref[pair:, :].astype(jnp.bfloat16)


def rest_kernel(
    place_ref, q_ref, do_ref, held_ref, dprobs_ref, q_in_ref, do_in_ref, held_in_ref,
    dprobs_in_ref, far_ref, near_ref, own_ref, dscores_ref, norm_ref,
    dq_ref, dq_send_ref, own_part_ref, window_ref, rows_ref, sem,
):
    core = place_ref[0]
    tokens = dq_send_ref.shape[0]
    kv_heads, lanes = q_ref.shape[:2]
    kv_width = kv_heads * HEAD_SIZE
    group = lanes // tokens
    scale = HEAD_SIZE ** (-0.5)
    pair = 2 * tokens
    for n, source in enumerate((far_ref, near_ref)):
        window_ref[n * pair : (n + 1) * pair, :] = source[:, :kv_width]
    store = pltpu.make_async_copy(rows_ref, dq_ref.at[core], sem)
    sides = (
        (1, dq_send_ref, q_in_ref, do_in_ref, held_in_ref, dprobs_in_ref),
        (0, rows_ref, q_ref, do_ref, held_ref, dprobs_ref),
    )
    for unit, target, q_side, do_side, held_side, dprobs_side in sides:
        first = unit * tokens
        before = 2 * pair - first
        reach = held_side.shape[1]
        for g in range(kv_heads):
            at = (g * HEAD_SIZE, kv_width + g * HEAD_SIZE)
            top, inverse = norm_ref[unit, g, 0:1], norm_ref[unit, g, 1:2]
            probs = jnp.exp2(held_side[g] - top) * inverse
            dscores = (probs * dprobs_side[g]).astype(jnp.bfloat16)
            keys = window_ref[first:, at[0] : at[0] + HEAD_SIZE]
            own_keys = own_ref[:reach, at[0] : at[0] + HEAD_SIZE]
            dq_t = dot(keys.T, dscores_ref[unit, g, :before]) + dot(own_keys.T, dscores)
            dq = (dq_t * scale).astype(jnp.bfloat16).T
            for a in range(group):
                column = (g * group + a) * HEAD_SIZE
                target[:, column : column + HEAD_SIZE] = dq[a * tokens : (a + 1) * tokens]
            if unit == 0 and g == kv_heads - 1:
                store.start()
            for part, column in (
                (dot(dscores, q_side[g]) * scale, at[0]),
                (dot(probs.astype(jnp.bfloat16), do_side[g]), at[1]),
            ):
                columns = slice(column, column + HEAD_SIZE)
                if unit == 1:
                    own_part_ref[:, columns] = part
                else:
                    own_part_ref[:reach, columns] += part
    store.wait()


def store_kernel(
    core_ref, rows_ref, kept_ref, given_ref, held_ref, dq_ref, key_ref, value_ref, sems
):
    core = core_ref[0]
    width = key_ref.shape[-1]
    copies = [pltpu.make_async_copy(rows_ref, dq_ref.at[1 - core], sems.at[0, 0])]
    for n, (source, slot) in enumerate(((kept_ref, core), (given_ref, 1 - core))):
        for m, target in enumerate((key_ref, value_ref)):
            copies.append(
                pltpu.make_async_copy(
                    source.at[:, pl.ds(m * width, width)], target.at[slot], sems.at[n + 1, m]
                )
            )
    for copy in copies:
        copy.start()
    for copy in copies:
        copy.wait()


def shards(query, key, value, out_grad, attn_out, doc_start):
    count = lax.axis_size("ctx")
    index = lax.axis_index("ctx")
    _, slots, tokens, width = query.shape
    kv_width = key.shape[-1]
    pair_width = 2 * kv_width
    pair = 2 * tokens
    core = (index % 2).astype(jnp.int32)
    stage = jnp.where(core == 0, index // 2, count - 1 - index // 2).astype(jnp.int32)
    core = core[None]
    place = jnp.stack([core[0], stage * pair])
    holder = [2 * s if 2 * s < count else 2 * count - 1 - 2 * s for s in range(count)]
    swap = [(i, i ^ 1) for i in range(count)]

    def shift(x, by):
        moves = [
            (holder[s], holder[s + by]) for s in range(count) if 0 <= s + by < count
        ]
        return lax.ppermute(x, "ctx", moves)

    bf16 = jnp.bfloat16
    def work(flops, moved):
        return pl.CostEstimate(flops=flops, bytes_accessed=moved, transcendentals=0)

    def swapped(x):
        return lax.ppermute(x, "ctx", swap)

    def mine(x):
        return jnp.where(core == 0, x[0], x[1])

    starts_in, key_in, value_in = (swapped(x[0]) for x in (doc_start, key, value))
    sides = ((key[0], value[0]), (key_in, value_in))
    own = jnp.concatenate(
        [jnp.concatenate([mine(x) for x in side], axis=-1) for side in sides], axis=0
    )
    own, starts_in, starts, *late = lax.optimization_barrier(
        (own, starts_in, doc_start[0], query[0], out_grad[0], attn_out[0])
    )
    kv_heads = kv_width // HEAD_SIZE
    lanes = tokens * (width // kv_width)
    products = 2 * slots * tokens * pair * width

    def arranged(unit, starts, sources):
        stacked = jax.ShapeDtypeStruct((kv_heads, lanes, HEAD_SIZE), bf16)
        square = jax.ShapeDtypeStruct((kv_heads, (unit + 1) * tokens, lanes), jnp.float32)
        q, do, scores, dprobs, delta = pl.pallas_call(
            functools.partial(rows_kernel, unit),
            out_shape=(
                stacked,
                stacked,
                square,
                square,
                jax.ShapeDtypeStruct((kv_heads, 8, lanes), jnp.float32),
            ),
            in_specs=[SMEM] + [VMEM] * 5,
            out_specs=(VMEM,) * 5,
            compiler_params=SMALL,
            cost_estimate=work(products // 2, 4 * 2**20),
            name="rows",
        )(place, starts, own, *sources)
        return (starts, q, do, scores, delta), (q, do, scores, dprobs)

    sent = [swapped(x) for x in late]
    far = shift(own, 2)
    near = shift(own, 1)
    side_in = arranged(1, starts_in, sent)
    *late, _ = lax.optimization_barrier((starts, *late, side_in[0][-1]))
    side = arranged(0, late[0], late[1:])
    far_part, near_part, dscores, norm = pl.pallas_call(
        scores_kernel,
        out_shape=(
            jax.ShapeDtypeStruct((pair, pair_width), bf16),
            jax.ShapeDtypeStruct((pair, pair_width), bf16),
            jax.ShapeDtypeStruct((slots, kv_heads, 2 * pair, lanes), bf16),
            jax.ShapeDtypeStruct((slots, kv_heads, 8, lanes), jnp.float32),
        ),
        in_specs=[SMEM] + [VMEM] * 12,
        out_specs=(VMEM,) * 4,
        scratch_shapes=[
            pltpu.VMEM((2 * pair, pair_width), bf16),
            pltpu.VMEM((2 * pair, pair_width), jnp.float32),
        ],
        compiler_params=PARAMS,
        cost_estimate=work(6 * products, 12 * 2**20),
        name="scores",
    )(place, *side[0], *side_in[0], far, near)
    from_far = shift(far_part, -2)
    from_near = shift(near_part, -1)
    dq, dq_send, own_part = pl.pallas_call(
        rest_kernel,
        out_shape=(
            jax.ShapeDtypeStruct((slots, tokens, width), bf16),
            jax.ShapeDtypeStruct((tokens, width), bf16),
            jax.ShapeDtypeStruct((pair, pair_width), jnp.float32),
        ),
        in_specs=[SMEM] + [VMEM] * 13,
        out_specs=(HBM, VMEM, VMEM),
        scratch_shapes=[
            pltpu.VMEM((2 * pair, kv_width), bf16),
            pltpu.VMEM((tokens, width), bf16),
            pltpu.SemaphoreType.DMA,
        ],
        compiler_params=PARAMS,
        cost_estimate=work(3 * products, 8 * 2**20),
        name="rest",
    )(place, *side[1], *side_in[1], far, near, own, dscores, norm)
    from_near, from_far, dq_send = lax.optimization_barrier((from_near, from_far, dq_send))
    dq_rows = swapped(dq_send)
    total = own_part + from_near.astype(jnp.float32) + from_far.astype(jnp.float32)
    total = total.astype(bf16)
    kept = total[:tokens]
    given = swapped(total[tokens:])
    dq, dk, dv = pl.pallas_call(
        store_kernel,
        out_shape=(
            jax.ShapeDtypeStruct(dq.shape, bf16),
            jax.ShapeDtypeStruct((slots, tokens, kv_width), bf16),
            jax.ShapeDtypeStruct((slots, tokens, kv_width), bf16),
        ),
        in_specs=[SMEM, VMEM, VMEM, VMEM, HBM],
        out_specs=(HBM,) * 3,
        scratch_shapes=[pltpu.SemaphoreType.DMA((3, 2))],
        input_output_aliases={4: 0},
        compiler_params=SMALL,
        name="store",
    )(core, dq_rows, kept, given, dq)
    return dq[None], dk[None], dv[None]


def solution(mesh):
    placed = (P("ctx", "dp", None, None),) * 5 + (P("ctx", "dp", None),)
    return jax.shard_map(
        shards,
        mesh=mesh,
        in_specs=placed,
        out_specs=(P("ctx", "dp", None, None),) * 3,
        check_vma=False,
    )
```

```python
import functools

import jax
import jax.numpy as jnp
from jax import lax
from jax.experimental import pallas as pl
from jax.experimental.pallas import tpu as pltpu
from jax.sharding import PartitionSpec as P

HEAD_SIZE = 128
STEPS = 4
LOG2E = 1.4426950408889634
CONTRACT_LAST = (((1,), (1,)), ((), ()))
CONTRACT_ROWS = (((1,), (0,)), ((), ()))
VMEM = pl.BlockSpec(memory_space=pltpu.VMEM)
SMEM = pl.BlockSpec(memory_space=pltpu.SMEM)
HBM = pl.BlockSpec(memory_space=pltpu.HBM)
PARAMS = pltpu.CompilerParams(vmem_limit_bytes=24 * 2**20)
SMALL = pltpu.CompilerParams(vmem_limit_bytes=4 * 2**20)


def dot(a, b, dims=CONTRACT_ROWS):
    return lax.dot_general(a, b, dims, preferred_element_type=jnp.float32)


def stack_heads(ref, first, count):
    return jnp.concatenate(
        [ref[:, (first + a) * HEAD_SIZE : (first + a + 1) * HEAD_SIZE] for a in range(count)],
        axis=0,
    )


def unit_starts(starts_ref, core):
    return jnp.where(core == 0, starts_ref[0:1, :], starts_ref[1:2, :])


def rows_kernel(
    unit, place_ref, starts_ref, own_ref, q_ref, do_ref, o_ref,
    q_out_ref, do_out_ref, scores_ref, dprobs_ref, delta_ref,
):
    core, begin = place_ref[0], place_ref[1]
    tokens = q_ref.shape[1]
    kv_heads, reach, lanes = scores_ref.shape
    kv_width = kv_heads * HEAD_SIZE
    group = lanes // tokens
    factor = HEAD_SIZE ** (-0.5) * LOG2E
    ones = jnp.ones((delta_ref.shape[1], 2 * HEAD_SIZE), jnp.bfloat16)
    low = unit_starts(starts_ref, core) - begin
    high = lax.broadcasted_iota(jnp.int32, (1, tokens), 1) + unit * tokens
    row = lax.broadcasted_iota(jnp.int32, (reach, tokens), 0)
    bias = jnp.where((row >= low) & (row <= high), 0.0, -jnp.inf)
    bias = jnp.concatenate([bias] * group, axis=1)
    for g in range(kv_heads):
        q, do, o = (
            stack_heads(r.at[core], g * group, group) for r in (q_ref, do_ref, o_ref)
        )
        keys = own_ref[:reach, g * HEAD_SIZE : (g + 1) * HEAD_SIZE]
        values = own_ref[:reach, kv_width + g * HEAD_SIZE : kv_width + (g + 1) * HEAD_SIZE]
        terms = do.astype(jnp.float32) * o.astype(jnp.float32)
        coarse = terms.astype(jnp.bfloat16)
        fine = (terms - coarse.astype(jnp.float32)).astype(jnp.bfloat16)
        delta = dot(ones, jnp.concatenate([coarse, fine], axis=1), CONTRACT_LAST)
        delta_ref[g] = delta
        scores_ref[g] = dot(keys, q, CONTRACT_LAST) * factor + bias
        dprobs_ref[g] = dot(values, do, CONTRACT_LAST) - delta[:1]
        q_out_ref[g] = q
        do_out_ref[g] = do


def remote_products(place_ref, side, pair_ref, unit, g, skip, offset):
    starts_ref, q_ref, do_ref, delta_ref = side
    core, begin = place_ref[0], place_ref[1]
    tokens = starts_ref.shape[1]
    kv_heads, lanes = q_ref.shape[:2]
    kv_width = kv_heads * HEAD_SIZE
    columns = slice(g * HEAD_SIZE, (g + 1) * HEAD_SIZE)
    values = pair_ref[skip:, kv_width + g * HEAD_SIZE : kv_width + (g + 1) * HEAD_SIZE]
    low = unit_starts(starts_ref, core) - (begin + (unit - STEPS) * tokens)
    low = jnp.maximum(lax.broadcasted_iota(jnp.int32, (1, tokens), 1) + 1, low) - offset
    low = jnp.concatenate([low] * (lanes // tokens), axis=1)
    factor = HEAD_SIZE ** (-0.5) * LOG2E
    scores = dot(pair_ref[skip:, columns], q_ref[g], CONTRACT_LAST) * factor
    row = lax.broadcasted_iota(jnp.int32, scores.shape, 0)
    scores = jnp.where(row >= low, scores, -jnp.inf)
    return scores, dot(values, do_ref[g], CONTRACT_LAST) - delta_ref[g, :1]


def far_kernel(
    place_ref, starts_ref, q_ref, do_ref, delta_ref,
    starts_in_ref, q_in_ref, do_in_ref, delta_in_ref, far_ref,
    scores_ref, dprobs_ref, scores_in_ref, dprobs_in_ref,
):
    tokens = starts_ref.shape[1]
    sides = (
        ((starts_ref, q_ref, do_ref, delta_ref), scores_ref, dprobs_ref),
        ((starts_in_ref, q_in_ref, do_in_ref, delta_in_ref), scores_in_ref, dprobs_in_ref),
    )
    for unit, (side, scores, dprobs) in enumerate(sides):
        for g in range(q_ref.shape[0]):
            scores[g], dprobs[g] = remote_products(
                place_ref, side, far_ref, unit, g, unit * tokens, 0
            )


def scores_kernel(
    place_ref, starts_ref, q_ref, do_ref, held_ref, delta_ref,
    starts_in_ref, q_in_ref, do_in_ref, held_in_ref, delta_in_ref,
    far_scores_ref, far_dprobs_ref, far_scores_in_ref, far_dprobs_in_ref, near_ref,
    far_part_ref, near_part_ref, dscores_ref, norm_ref, part_ref,
):
    tokens = starts_ref.shape[1]
    kv_heads = q_ref.shape[0]
    kv_width = kv_heads * HEAD_SIZE
    scale = HEAD_SIZE ** (-0.5)
    pair = 2 * tokens
    sides = (
        (starts_ref, q_ref, do_ref, delta_ref),
        (starts_in_ref, q_in_ref, do_in_ref, delta_in_ref),
    )
    known = (
        (held_ref, far_scores_ref, far_dprobs_ref),
        (held_in_ref, far_scores_in_ref, far_dprobs_in_ref),
    )

    def products(unit, g):
        return remote_products(place_ref, sides[unit], near_ref, unit, g, 0, pair - unit * tokens)

    order = [(unit, g) for unit in range(2) for g in range(kv_heads)]
    ahead = products(*order[0])
    for step, (unit, g) in enumerate(order):
        near_scores, near_dprobs = ahead
        if step + 1 < len(order):
            ahead = products(*order[step + 1])
        q, do = sides[unit][1][g], sides[unit][2][g]
        held, far_scores, far_dprobs = (r[g] for r in known[unit])
        first = unit * tokens
        split, before = pair - first, 2 * pair - first
        groups = (held, far_scores, near_scores)
        tops = [jnp.max(x, axis=0, keepdims=True) for x in groups]
        top = jnp.maximum(jnp.maximum(tops[0], tops[1]), tops[2])
        own, far, near = (jnp.exp2(x - top) for x in groups)
        inverse = 1.0 / sum(jnp.sum(x, axis=0, keepdims=True) for x in (own, far, near))
        norm_ref[unit, g, 0:1] = top
        norm_ref[unit, g, 1:2] = inverse
        parts = (
            (far * inverse, far_dprobs, slice(0, split), slice(first, pair)),
            (near * inverse, near_dprobs, slice(split, before), slice(pair, 2 * pair)),
        )
        for probs, dprobs, window_rows, pair_rows in parts:
            dscores = (probs * dprobs).astype(jnp.bfloat16)
            dscores_ref[unit, g, window_rows] = dscores
            for part, column in (
                (dot(dscores, q) * scale, g * HEAD_SIZE),
                (dot(probs.astype(jnp.bfloat16), do), kv_width + g * HEAD_SIZE),
            ):
                columns = slice(column, column + HEAD_SIZE)
                if unit == 0:
                    part_ref[pair_rows, columns] = part
                else:
                    part_ref[pair_rows, columns] += part
    far_part_ref[...] = part_ref[:pair, :].astype(jnp.bfloat16)
    near_part_ref[...] = part_ref[pair:, :].astype(jnp.bfloat16)


def rest_kernel(
    place_ref, q_ref, do_ref, held_ref, dprobs_ref, q_in_ref, do_in_ref, held_in_ref,
    dprobs_in_ref, far_ref, near_ref, own_ref, dscores_ref, norm_ref,
    dq_ref, dq_send_ref, own_part_ref, window_ref, rows_ref, sem,
):
    core = place_ref[0]
    tokens = dq_send_ref.shape[0]
    kv_heads, lanes = q_ref.shape[:2]
    kv_width = kv_heads * HEAD_SIZE
    group = lanes // tokens
    scale = HEAD_SIZE ** (-0.5)
    pair = 2 * tokens
    for n, source in enumerate((far_ref, near_ref)):
        window_ref[n * pair : (n + 1) * pair, :] = source[:, :kv_width]
    store = pltpu.make_async_copy(rows_ref, dq_ref.at[core], sem)
    sides = (
        (1, dq_send_ref, q_in_ref, do_in_ref, held_in_ref, dprobs_in_ref),
        (0, rows_ref, q_ref, do_ref, held_ref, dprobs_ref),
    )
    for unit, target, q_side, do_side, held_side, dprobs_side in sides:
        first = unit * tokens
        before = 2 * pair - first
        reach = held_side.shape[1]
        for g in range(kv_heads):
            at = (g * HEAD_SIZE, kv_width + g * HEAD_SIZE)
            top, inverse = norm_ref[unit, g, 0:1], norm_ref[unit, g, 1:2]
            probs = jnp.exp2(held_side[g] - top) * inverse
            dscores = (probs * dprobs_side[g]).astype(jnp.bfloat16)
            keys = window_ref[first:, at[0] : at[0] + HEAD_SIZE]
            own_keys = own_ref[:reach, at[0] : at[0] + HEAD_SIZE]
            dq_t = dot(keys.T, dscores_ref[unit, g, :before]) + dot(own_keys.T, dscores)
            dq = (dq_t * scale).astype(jnp.bfloat16).T
            for a in range(group):
                column = (g * group + a) * HEAD_SIZE
                target[:, column : column + HEAD_SIZE] = dq[a * tokens : (a + 1) * tokens]
            if unit == 0 and g == kv_heads - 1:
                store.start()
            for part, column in (
                (dot(dscores, q_side[g]) * scale, at[0]),
                (dot(probs.astype(jnp.bfloat16), do_side[g]), at[1]),
            ):
                columns = slice(column, column + HEAD_SIZE)
                if unit == 1:
                    own_part_ref[:, columns] = part
                else:
                    own_part_ref[:reach, columns] += part
    store.wait()


def store_kernel(
    core_ref, rows_ref, kept_ref, given_ref, held_ref, dq_ref, key_ref, value_ref, sems
):
    core = core_ref[0]
    width = key_ref.shape[-1]
    copies = [pltpu.make_async_copy(rows_ref, dq_ref.at[1 - core], sems.at[0, 0])]
    for n, (source, slot) in enumerate(((kept_ref, core), (given_ref, 1 - core))):
        for m, target in enumerate((key_ref, value_ref)):
            copies.append(
                pltpu.make_async_copy(
                    source.at[:, pl.ds(m * width, width)], target.at[slot], sems.at[n + 1, m]
                )
            )
    for copy in copies:
        copy.start()
    for copy in copies:
        copy.wait()


def shards(query, key, value, out_grad, attn_out, doc_start):
    count = lax.axis_size("ctx")
    index = lax.axis_index("ctx")
    _, slots, tokens, width = query.shape
    kv_width = key.shape[-1]
    pair_width = 2 * kv_width
    pair = 2 * tokens
    core = (index % 2).astype(jnp.int32)
    stage = jnp.where(core == 0, index // 2, count - 1 - index // 2).astype(jnp.int32)
    core = core[None]
    place = jnp.stack([core[0], stage * pair])
    holder = [2 * s if 2 * s < count else 2 * count - 1 - 2 * s for s in range(count)]
    swap = [(i, i ^ 1) for i in range(count)]

    def shift(x, by):
        moves = [
            (holder[s], holder[s + by]) for s in range(count) if 0 <= s + by < count
        ]
        return lax.ppermute(x, "ctx", moves)

    bf16 = jnp.bfloat16
    def work(flops, moved):
        return pl.CostEstimate(flops=flops, bytes_accessed=moved, transcendentals=0)

    def swapped(x):
        return lax.ppermute(x, "ctx", swap)

    def mine(x):
        return jnp.where(core == 0, x[0], x[1])

    starts_in, key_in, value_in = (swapped(x[0]) for x in (doc_start, key, value))
    sides = ((key[0], value[0]), (key_in, value_in))
    own = jnp.concatenate(
        [jnp.concatenate([mine(x) for x in side], axis=-1) for side in sides], axis=0
    )
    own, starts_in, starts, *late = lax.optimization_barrier(
        (own, starts_in, doc_start[0], query[0], out_grad[0], attn_out[0])
    )
    kv_heads = kv_width // HEAD_SIZE
    lanes = tokens * (width // kv_width)
    products = 2 * slots * tokens * pair * width

    def arranged(unit, starts, sources):
        stacked = jax.ShapeDtypeStruct((kv_heads, lanes, HEAD_SIZE), bf16)
        square = jax.ShapeDtypeStruct((kv_heads, (unit + 1) * tokens, lanes), jnp.float32)
        q, do, scores, dprobs, delta = pl.pallas_call(
            functools.partial(rows_kernel, unit),
            out_shape=(
                stacked,
                stacked,
                square,
                square,
                jax.ShapeDtypeStruct((kv_heads, 8, lanes), jnp.float32),
            ),
            in_specs=[SMEM] + [VMEM] * 5,
            out_specs=(VMEM,) * 5,
            compiler_params=SMALL,
            cost_estimate=work(products // 2, 4 * 2**20),
            name="rows",
        )(place, starts, own, *sources)
        return (starts, q, do, scores, delta), (q, do, scores, dprobs)

    sent = [swapped(x) for x in late]
    far = shift(own, 2)
    near = shift(own, 1)
    side_in = arranged(1, starts_in, sent)
    *late, _ = lax.optimization_barrier((starts, *late, side_in[0][-1]))
    side = arranged(0, late[0], late[1:])
    def remote(rows):
        return jax.ShapeDtypeStruct((kv_heads, rows, lanes), jnp.float32)

    far_products = pl.pallas_call(
        far_kernel,
        out_shape=(remote(pair), remote(pair), remote(tokens), remote(tokens)),
        in_specs=[SMEM] + [VMEM] * 9,
        out_specs=(VMEM,) * 4,
        compiler_params=SMALL,
        cost_estimate=work(2 * products, 4 * 2**20),
        name="far_scores",
    )(place, *(x for part in (side[0], side_in[0]) for x in part[:3] + part[4:]), far)
    far_part, near_part, dscores, norm = pl.pallas_call(
        scores_kernel,
        out_shape=(
            jax.ShapeDtypeStruct((pair, pair_width), bf16),
            jax.ShapeDtypeStruct((pair, pair_width), bf16),
            jax.ShapeDtypeStruct((slots, kv_heads, 2 * pair, lanes), bf16),
            jax.ShapeDtypeStruct((slots, kv_heads, 8, lanes), jnp.float32),
        ),
        in_specs=[SMEM] + [VMEM] * 15,
        out_specs=(VMEM,) * 4,
        scratch_shapes=[pltpu.VMEM((2 * pair, pair_width), jnp.float32)],
        compiler_params=PARAMS,
        cost_estimate=work(6 * products, 12 * 2**20),
        name="scores",
    )(place, *side[0], *side_in[0], *far_products, near)
    from_far = shift(far_part, -2)
    from_near = shift(near_part, -1)
    dq, dq_send, own_part = pl.pallas_call(
        rest_kernel,
        out_shape=(
            jax.ShapeDtypeStruct((slots, tokens, width), bf16),
            jax.ShapeDtypeStruct((tokens, width), bf16),
            jax.ShapeDtypeStruct((pair, pair_width), jnp.float32),
        ),
        in_specs=[SMEM] + [VMEM] * 13,
        out_specs=(HBM, VMEM, VMEM),
        scratch_shapes=[
            pltpu.VMEM((2 * pair, kv_width), bf16),
            pltpu.VMEM((tokens, width), bf16),
            pltpu.SemaphoreType.DMA,
        ],
        compiler_params=PARAMS,
        cost_estimate=work(3 * products, 8 * 2**20),
        name="rest",
    )(place, *side[1], *side_in[1], far, near, own, dscores, norm)
    from_near, from_far, dq_send = lax.optimization_barrier((from_near, from_far, dq_send))
    dq_rows = swapped(dq_send)
    total = own_part + from_near.astype(jnp.float32) + from_far.astype(jnp.float32)
    total = total.astype(bf16)
    kept = total[:tokens]
    given = swapped(total[tokens:])
    dq, dk, dv = pl.pallas_call(
        store_kernel,
        out_shape=(
            jax.ShapeDtypeStruct(dq.shape, bf16),
            jax.ShapeDtypeStruct((slots, tokens, kv_width), bf16),
            jax.ShapeDtypeStruct((slots, tokens, kv_width), bf16),
        ),
        in_specs=[SMEM, VMEM, VMEM, VMEM, HBM],
        out_specs=(HBM,) * 3,
        scratch_shapes=[pltpu.SemaphoreType.DMA((3, 2))],
        input_output_aliases={4: 0},
        compiler_params=SMALL,
        name="store",
    )(core, dq_rows, kept, given, dq)
    return dq[None], dk[None], dv[None]


def solution(mesh):
    placed = (P("ctx", "dp", None, None),) * 5 + (P("ctx", "dp", None),)
    return jax.shard_map(
        shards,
        mesh=mesh,
        in_specs=placed,
        out_specs=(P("ctx", "dp", None, None),) * 3,
        check_vma=False,
    )
```

```python
import functools

import jax
import jax.numpy as jnp
from jax import lax
from jax.experimental import pallas as pl
from jax.experimental.pallas import tpu as pltpu
from jax.sharding import PartitionSpec as P

HEAD_SIZE = 128
STEPS = 4
LOG2E = 1.4426950408889634
CONTRACT_LAST = (((1,), (1,)), ((), ()))
CONTRACT_ROWS = (((1,), (0,)), ((), ()))
VMEM = pl.BlockSpec(memory_space=pltpu.VMEM)
SMEM = pl.BlockSpec(memory_space=pltpu.SMEM)
HBM = pl.BlockSpec(memory_space=pltpu.HBM)
PARAMS = pltpu.CompilerParams(vmem_limit_bytes=24 * 2**20)
SMALL = pltpu.CompilerParams(vmem_limit_bytes=4 * 2**20)


def dot(a, b, dims=CONTRACT_ROWS):
    return lax.dot_general(a, b, dims, preferred_element_type=jnp.float32)


def stack_heads(ref, first, count):
    return jnp.concatenate(
        [ref[:, (first + a) * HEAD_SIZE : (first + a + 1) * HEAD_SIZE] for a in range(count)],
        axis=0,
    )


def unit_starts(starts_ref, core):
    return jnp.where(core == 0, starts_ref[0:1, :], starts_ref[1:2, :])


def rows_kernel(
    unit, place_ref, starts_ref, own_ref, q_ref, do_ref, o_ref,
    q_out_ref, do_out_ref, scores_ref, dprobs_ref, delta_ref,
):
    core, begin = place_ref[0], place_ref[1]
    tokens = q_ref.shape[1]
    kv_heads, reach, lanes = scores_ref.shape
    kv_width = kv_heads * HEAD_SIZE
    group = lanes // tokens
    factor = HEAD_SIZE ** (-0.5) * LOG2E
    ones = jnp.ones((delta_ref.shape[1], 2 * HEAD_SIZE), jnp.bfloat16)
    low = unit_starts(starts_ref, core) - begin
    high = lax.broadcasted_iota(jnp.int32, (1, tokens), 1) + unit * tokens
    row = lax.broadcasted_iota(jnp.int32, (reach, tokens), 0)
    bias = jnp.where((row >= low) & (row <= high), 0.0, -jnp.inf)
    bias = jnp.concatenate([bias] * group, axis=1)
    for g in range(kv_heads):
        q, do, o = (
            stack_heads(r.at[core], g * group, group) for r in (q_ref, do_ref, o_ref)
        )
        keys = own_ref[:reach, g * HEAD_SIZE : (g + 1) * HEAD_SIZE]
        values = own_ref[:reach, kv_width + g * HEAD_SIZE : kv_width + (g + 1) * HEAD_SIZE]
        terms = do.astype(jnp.float32) * o.astype(jnp.float32)
        coarse = terms.astype(jnp.bfloat16)
        fine = (terms - coarse.astype(jnp.float32)).astype(jnp.bfloat16)
        delta = dot(ones, jnp.concatenate([coarse, fine], axis=1), CONTRACT_LAST)
        delta_ref[g] = delta
        scores_ref[g] = dot(keys, q, CONTRACT_LAST) * factor + bias
        dprobs_ref[g] = dot(values, do, CONTRACT_LAST) - delta[:1]
        q_out_ref[g] = q
        do_out_ref[g] = do


def scores_kernel(
    place_ref, starts_ref, q_ref, do_ref, held_ref, delta_ref,
    starts_in_ref, q_in_ref, do_in_ref, held_in_ref, delta_in_ref, far_ref, near_ref,
    far_part_ref, near_part_ref, dscores_ref, norm_ref, window_ref, part_ref,
):
    core, begin = place_ref[0], place_ref[1]
    tokens = starts_ref.shape[1]
    kv_heads, lanes = q_ref.shape[:2]
    kv_width = kv_heads * HEAD_SIZE
    group = lanes // tokens
    scale = HEAD_SIZE ** (-0.5)
    pair = 2 * tokens
    for n, source in enumerate((far_ref, near_ref)):
        window_ref[n * pair : (n + 1) * pair, :] = source[...]
    offset = lax.broadcasted_iota(jnp.int32, (1, tokens), 1)
    sides = (
        (starts_ref, q_ref, do_ref, held_ref, delta_ref),
        (starts_in_ref, q_in_ref, do_in_ref, held_in_ref, delta_in_ref),
    )

    def products(unit, g):
        starts, q_side, do_side, held_side, delta_side = sides[unit]
        first = unit * tokens
        columns = slice(g * HEAD_SIZE, (g + 1) * HEAD_SIZE)
        values = window_ref[first:, kv_width + g * HEAD_SIZE : kv_width + (g + 1) * HEAD_SIZE]
        low = unit_starts(starts, core) - (begin + (unit - STEPS) * tokens)
        low = jnp.concatenate([jnp.maximum(offset + 1, low)] * group, axis=1)
        scores = dot(window_ref[first:, columns], q_side[g], CONTRACT_LAST) * (scale * LOG2E)
        row = lax.broadcasted_iota(jnp.int32, scores.shape, 0)
        scores = jnp.where(row >= low, scores, -jnp.inf)
        return scores, dot(values, do_side[g], CONTRACT_LAST)

    order = [(unit, g) for unit in range(2) for g in range(kv_heads)]
    ahead = products(*order[0])
    for step, (unit, g) in enumerate(order):
        scores, dprobs = ahead
        if step + 1 < len(order):
            ahead = products(*order[step + 1])
        _, q_side, do_side, held_side, delta_side = sides[unit]
        first = unit * tokens
        before = 2 * pair - first
        held = held_side[g]
        top = jnp.maximum(
            jnp.max(scores, axis=0, keepdims=True), jnp.max(held, axis=0, keepdims=True)
        )
        weights = jnp.exp2(scores - top)
        total = jnp.sum(weights, axis=0, keepdims=True)
        total += jnp.sum(jnp.exp2(held - top), axis=0, keepdims=True)
        inverse = 1.0 / total
        probs = weights * inverse
        norm_ref[unit, g, 0:1] = top
        norm_ref[unit, g, 1:2] = inverse
        dscores = (probs * (dprobs - delta_side[g, :1])).astype(jnp.bfloat16)
        dscores_ref[unit, g, :before] = dscores
        for part, column in (
            (dot(dscores, q_side[g]) * scale, g * HEAD_SIZE),
            (dot(probs.astype(jnp.bfloat16), do_side[g]), kv_width + g * HEAD_SIZE),
        ):
            columns = slice(column, column + HEAD_SIZE)
            if unit == 0:
                part_ref[:, columns] = part
            else:
                part_ref[first:, columns] += part
    far_part_ref[...] = part_ref[:pair, :].astype(jnp.bfloat16)
    near_part_ref[...] = part_ref[pair:, :].astype(jnp.bfloat16)


def rest_kernel(
    place_ref, q_ref, do_ref, held_ref, dprobs_ref, q_in_ref, do_in_ref, held_in_ref,
    dprobs_in_ref, far_ref, near_ref, own_ref, dscores_ref, norm_ref,
    dq_ref, dq_send_ref, own_part_ref, window_ref, rows_ref, sem,
):
    core = place_ref[0]
    tokens = dq_send_ref.shape[0]
    kv_heads, lanes = q_ref.shape[:2]
    kv_width = kv_heads * HEAD_SIZE
    group = lanes // tokens
    scale = HEAD_SIZE ** (-0.5)
    pair = 2 * tokens
    for n, source in enumerate((far_ref, near_ref)):
        window_ref[n * pair : (n + 1) * pair, :] = source[:, :kv_width]
    store = pltpu.make_async_copy(rows_ref, dq_ref.at[core], sem)
    sides = (
        (1, dq_send_ref, q_in_ref, do_in_ref, held_in_ref, dprobs_in_ref),
        (0, rows_ref, q_ref, do_ref, held_ref, dprobs_ref),
    )
    for unit, target, q_side, do_side, held_side, dprobs_side in sides:
        first = unit * tokens
        before = 2 * pair - first
        reach = held_side.shape[1]
        for g in range(kv_heads):
            at = (g * HEAD_SIZE, kv_width + g * HEAD_SIZE)
            top, inverse = norm_ref[unit, g, 0:1], norm_ref[unit, g, 1:2]
            probs = jnp.exp2(held_side[g] - top) * inverse
            dscores = (probs * dprobs_side[g]).astype(jnp.bfloat16)
            keys = window_ref[first:, at[0] : at[0] + HEAD_SIZE]
            own_keys = own_ref[:reach, at[0] : at[0] + HEAD_SIZE]
            dq_t = dot(keys.T, dscores_ref[unit, g, :before]) + dot(own_keys.T, dscores)
            dq = (dq_t * scale).astype(jnp.bfloat16).T
            for a in range(group):
                column = (g * group + a) * HEAD_SIZE
                target[:, column : column + HEAD_SIZE] = dq[a * tokens : (a + 1) * tokens]
            if unit == 0 and g == kv_heads - 1:
                store.start()
            for part, column in (
                (dot(dscores, q_side[g]) * scale, at[0]),
                (dot(probs.astype(jnp.bfloat16), do_side[g]), at[1]),
            ):
                columns = slice(column, column + HEAD_SIZE)
                if unit == 1:
                    own_part_ref[:, columns] = part
                else:
                    own_part_ref[:reach, columns] += part
    store.wait()


def store_kernel(
    core_ref, rows_ref, kept_ref, given_ref, held_ref, dq_ref, key_ref, value_ref, sems
):
    core = core_ref[0]
    width = key_ref.shape[-1]
    copies = [pltpu.make_async_copy(rows_ref, dq_ref.at[1 - core], sems.at[0, 0])]
    for n, (source, slot) in enumerate(((kept_ref, core), (given_ref, 1 - core))):
        for m, target in enumerate((key_ref, value_ref)):
            copies.append(
                pltpu.make_async_copy(
                    source.at[:, pl.ds(m * width, width)], target.at[slot], sems.at[n + 1, m]
                )
            )
    for copy in copies:
        copy.start()
    for copy in copies:
        copy.wait()


def shards(query, key, value, out_grad, attn_out, doc_start):
    count = lax.axis_size("ctx")
    index = lax.axis_index("ctx")
    _, slots, tokens, width = query.shape
    kv_width = key.shape[-1]
    pair_width = 2 * kv_width
    pair = 2 * tokens
    core = (index % 2).astype(jnp.int32)
    stage = jnp.where(core == 0, index // 2, count - 1 - index // 2).astype(jnp.int32)
    core = core[None]
    place = jnp.stack([core[0], stage * pair])
    holder = [2 * s if 2 * s < count else 2 * count - 1 - 2 * s for s in range(count)]
    swap = [(i, i ^ 1) for i in range(count)]

    def shift(x, by):
        moves = [
            (holder[s], holder[s + by]) for s in range(count) if 0 <= s + by < count
        ]
        return lax.ppermute(x, "ctx", moves)

    bf16 = jnp.bfloat16
    def work(flops, moved):
        return pl.CostEstimate(flops=flops, bytes_accessed=moved, transcendentals=0)

    def swapped(x):
        return lax.ppermute(x, "ctx", swap)

    def mine(x):
        return jnp.where(core == 0, x[0], x[1])

    starts_in, key_in, value_in = (swapped(x[0]) for x in (doc_start, key, value))
    key_in, *late = lax.optimization_barrier((key_in, query[0], out_grad[0], attn_out[0]))
    sent = [swapped(x) for x in late]
    sides = ((key[0], value[0]), (key_in, value_in))
    own = jnp.concatenate(
        [jnp.concatenate([mine(x) for x in side], axis=-1) for side in sides], axis=0
    )
    own, starts_in, starts = lax.optimization_barrier((own, starts_in, doc_start[0]))
    kv_heads = kv_width // HEAD_SIZE
    lanes = tokens * (width // kv_width)
    products = 2 * slots * tokens * pair * width

    def arranged(unit, starts, sources):
        stacked = jax.ShapeDtypeStruct((kv_heads, lanes, HEAD_SIZE), bf16)
        square = jax.ShapeDtypeStruct((kv_heads, (unit + 1) * tokens, lanes), jnp.float32)
        q, do, scores, dprobs, delta = pl.pallas_call(
            functools.partial(rows_kernel, unit),
            out_shape=(
                stacked,
                stacked,
                square,
                square,
                jax.ShapeDtypeStruct((kv_heads, 8, lanes), jnp.float32),
            ),
            in_specs=[SMEM] + [VMEM] * 5,
            out_specs=(VMEM,) * 5,
            compiler_params=SMALL,
            cost_estimate=work(products // 2, 4 * 2**20),
            name="rows",
        )(place, starts, own, *sources)
        return (starts, q, do, scores, delta), (q, do, scores, dprobs)

    far = shift(own, 2)
    near = shift(own, 1)
    side_in = arranged(1, starts_in, sent)
    *late, _ = lax.optimization_barrier((starts, *late, side_in[0][-1]))
    side = arranged(0, late[0], late[1:])
    far_part, near_part, dscores, norm = pl.pallas_call(
        scores_kernel,
        out_shape=(
            jax.ShapeDtypeStruct((pair, pair_width), bf16),
            jax.ShapeDtypeStruct((pair, pair_width), bf16),
            jax.ShapeDtypeStruct((slots, kv_heads, 2 * pair, lanes), bf16),
            jax.ShapeDtypeStruct((slots, kv_heads, 8, lanes), jnp.float32),
        ),
        in_specs=[SMEM] + [VMEM] * 12,
        out_specs=(VMEM,) * 4,
        scratch_shapes=[
            pltpu.VMEM((2 * pair, pair_width), bf16),
            pltpu.VMEM((2 * pair, pair_width), jnp.float32),
        ],
        compiler_params=PARAMS,
        cost_estimate=work(6 * products, 12 * 2**20),
        name="scores",
    )(place, *side[0], *side_in[0], far, near)
    from_far = shift(far_part, -2)
    from_near = shift(near_part, -1)
    dq, dq_send, own_part = pl.pallas_call(
        rest_kernel,
        out_shape=(
            jax.ShapeDtypeStruct((slots, tokens, width), bf16),
            jax.ShapeDtypeStruct((tokens, width), bf16),
            jax.ShapeDtypeStruct((pair, pair_width), jnp.float32),
        ),
        in_specs=[SMEM] + [VMEM] * 13,
        out_specs=(HBM, VMEM, VMEM),
        scratch_shapes=[
            pltpu.VMEM((2 * pair, kv_width), bf16),
            pltpu.VMEM((tokens, width), bf16),
            pltpu.SemaphoreType.DMA,
        ],
        compiler_params=PARAMS,
        cost_estimate=work(3 * products, 8 * 2**20),
        name="rest",
    )(place, *side[1], *side_in[1], far, near, own, dscores, norm)
    from_near, from_far, dq_send = lax.optimization_barrier((from_near, from_far, dq_send))
    dq_rows = swapped(dq_send)
    total = own_part + from_near.astype(jnp.float32) + from_far.astype(jnp.float32)
    total = total.astype(bf16)
    kept = total[:tokens]
    given = swapped(total[tokens:])
    dq, dk, dv = pl.pallas_call(
        store_kernel,
        out_shape=(
            jax.ShapeDtypeStruct(dq.shape, bf16),
            jax.ShapeDtypeStruct((slots, tokens, kv_width), bf16),
            jax.ShapeDtypeStruct((slots, tokens, kv_width), bf16),
        ),
        in_specs=[SMEM, VMEM, VMEM, VMEM, HBM],
        out_specs=(HBM,) * 3,
        scratch_shapes=[pltpu.SemaphoreType.DMA((3, 2))],
        input_output_aliases={4: 0},
        compiler_params=SMALL,
        name="store",
    )(core, dq_rows, kept, given, dq)
    return dq[None], dk[None], dv[None]


def solution(mesh):
    placed = (P("ctx", "dp", None, None),) * 5 + (P("ctx", "dp", None),)
    return jax.shard_map(
        shards,
        mesh=mesh,
        in_specs=placed,
        out_specs=(P("ctx", "dp", None, None),) * 3,
        check_vma=False,
    )
```

```python
import functools

import jax
import jax.numpy as jnp
from jax import lax
from jax.experimental import pallas as pl
from jax.experimental.pallas import tpu as pltpu
from jax.sharding import PartitionSpec as P

HEAD_SIZE = 128
STEPS = 4
LOG2E = 1.4426950408889634
CONTRACT_LAST = (((1,), (1,)), ((), ()))
CONTRACT_ROWS = (((1,), (0,)), ((), ()))
VMEM = pl.BlockSpec(memory_space=pltpu.VMEM)
SMEM = pl.BlockSpec(memory_space=pltpu.SMEM)
HBM = pl.BlockSpec(memory_space=pltpu.HBM)
PARAMS = pltpu.CompilerParams(vmem_limit_bytes=24 * 2**20)
SMALL = pltpu.CompilerParams(vmem_limit_bytes=4 * 2**20)


def dot(a, b, dims=CONTRACT_ROWS):
    return lax.dot_general(a, b, dims, preferred_element_type=jnp.float32)


def stack_heads(ref, first, count):
    return jnp.concatenate(
        [ref[:, (first + a) * HEAD_SIZE : (first + a + 1) * HEAD_SIZE] for a in range(count)],
        axis=0,
    )


def unit_starts(starts_ref, core):
    return jnp.where(core == 0, starts_ref[0:1, :], starts_ref[1:2, :])


def rows_kernel(
    unit, place_ref, starts_ref, own_ref, q_ref, do_ref, o_ref,
    q_out_ref, do_out_ref, scores_ref, dprobs_ref, delta_ref,
):
    core, begin = place_ref[0], place_ref[1]
    tokens = q_ref.shape[1]
    kv_heads, reach, lanes = scores_ref.shape
    kv_width = kv_heads * HEAD_SIZE
    group = lanes // tokens
    factor = HEAD_SIZE ** (-0.5) * LOG2E
    ones = jnp.ones((delta_ref.shape[1], 2 * HEAD_SIZE), jnp.bfloat16)
    low = unit_starts(starts_ref, core) - begin
    high = lax.broadcasted_iota(jnp.int32, (1, tokens), 1) + unit * tokens
    row = lax.broadcasted_iota(jnp.int32, (reach, tokens), 0)
    bias = jnp.where((row >= low) & (row <= high), 0.0, -jnp.inf)
    bias = jnp.concatenate([bias] * group, axis=1)
    for g in range(kv_heads):
        q, do, o = (
            stack_heads(r.at[core], g * group, group) for r in (q_ref, do_ref, o_ref)
        )
        keys = own_ref[:reach, g * HEAD_SIZE : (g + 1) * HEAD_SIZE]
        values = own_ref[:reach, kv_width + g * HEAD_SIZE : kv_width + (g + 1) * HEAD_SIZE]
        terms = do.astype(jnp.float32) * o.astype(jnp.float32)
        coarse = terms.astype(jnp.bfloat16)
        fine = (terms - coarse.astype(jnp.float32)).astype(jnp.bfloat16)
        delta = dot(ones, jnp.concatenate([coarse, fine], axis=1), CONTRACT_LAST)
        delta_ref[g] = delta
        scores_ref[g] = dot(keys, q, CONTRACT_LAST) * factor + bias
        dprobs_ref[g] = dot(values, do, CONTRACT_LAST) - delta[:1]
        q_out_ref[g] = q
        do_out_ref[g] = do


def scores_kernel(
    place_ref, starts_ref, q_ref, do_ref, held_ref, delta_ref,
    starts_in_ref, q_in_ref, do_in_ref, held_in_ref, delta_in_ref, far_ref, near_ref,
    far_part_ref, near_part_ref, dscores_ref, norm_ref, window_ref, part_ref,
):
    core, begin = place_ref[0], place_ref[1]
    tokens = starts_ref.shape[1]
    kv_heads, lanes = q_ref.shape[:2]
    kv_width = kv_heads * HEAD_SIZE
    group = lanes // tokens
    scale = HEAD_SIZE ** (-0.5)
    pair = 2 * tokens
    for n, source in enumerate((far_ref, near_ref)):
        window_ref[n * pair : (n + 1) * pair, :] = source[...]
    offset = lax.broadcasted_iota(jnp.int32, (1, tokens), 1)
    sides = (
        (starts_ref, q_ref, do_ref, held_ref, delta_ref),
        (starts_in_ref, q_in_ref, do_in_ref, held_in_ref, delta_in_ref),
    )

    def products(unit, g):
        starts, q_side, do_side, held_side, delta_side = sides[unit]
        first = unit * tokens
        columns = slice(g * HEAD_SIZE, (g + 1) * HEAD_SIZE)
        values = window_ref[first:, kv_width + g * HEAD_SIZE : kv_width + (g + 1) * HEAD_SIZE]
        low = unit_starts(starts, core) - (begin + (unit - STEPS) * tokens)
        low = jnp.concatenate([jnp.maximum(offset + 1, low)] * group, axis=1)
        scores = dot(window_ref[first:, columns], q_side[g], CONTRACT_LAST) * (scale * LOG2E)
        row = lax.broadcasted_iota(jnp.int32, scores.shape, 0)
        scores = jnp.where(row >= low, scores, -jnp.inf)
        return scores, dot(values, do_side[g], CONTRACT_LAST)

    order = [(unit, g) for unit in range(2) for g in range(kv_heads)]
    ahead = products(*order[0])
    for step, (unit, g) in enumerate(order):
        scores, dprobs = ahead
        if step + 1 < len(order):
            ahead = products(*order[step + 1])
        _, q_side, do_side, held_side, delta_side = sides[unit]
        first = unit * tokens
        before = 2 * pair - first
        held = held_side[g]
        top = jnp.maximum(
            jnp.max(scores, axis=0, keepdims=True), jnp.max(held, axis=0, keepdims=True)
        )
        weights = jnp.exp2(scores - top)
        total = jnp.sum(weights, axis=0, keepdims=True)
        total += jnp.sum(jnp.exp2(held - top), axis=0, keepdims=True)
        inverse = 1.0 / total
        probs = weights * inverse
        norm_ref[unit, g, 0:1] = top
        norm_ref[unit, g, 1:2] = inverse
        dscores = (probs * (dprobs - delta_side[g, :1])).astype(jnp.bfloat16)
        dscores_ref[unit, g, :before] = dscores
        for part, column in (
            (dot(dscores, q_side[g]) * scale, g * HEAD_SIZE),
            (dot(probs.astype(jnp.bfloat16), do_side[g]), kv_width + g * HEAD_SIZE),
        ):
            columns = slice(column, column + HEAD_SIZE)
            if unit == 0:
                part_ref[:, columns] = part
            else:
                part_ref[first:, columns] += part
    far_part_ref[...] = part_ref[:pair, :].astype(jnp.bfloat16)
    near_part_ref[...] = part_ref[pair:, :].astype(jnp.bfloat16)


def rest_kernel(
    place_ref, q_ref, do_ref, held_ref, dprobs_ref, q_in_ref, do_in_ref, held_in_ref,
    dprobs_in_ref, far_ref, near_ref, own_ref, dscores_ref, norm_ref,
    dq_ref, dq_send_ref, own_part_ref, window_ref, rows_ref, sem,
):
    core = place_ref[0]
    tokens = dq_send_ref.shape[0]
    kv_heads, lanes = q_ref.shape[:2]
    kv_width = kv_heads * HEAD_SIZE
    group = lanes // tokens
    scale = HEAD_SIZE ** (-0.5)
    pair = 2 * tokens
    for n, source in enumerate((far_ref, near_ref)):
        window_ref[n * pair : (n + 1) * pair, :] = source[:, :kv_width]
    store = pltpu.make_async_copy(rows_ref, dq_ref.at[core], sem)
    sides = (
        (1, dq_send_ref, q_in_ref, do_in_ref, held_in_ref, dprobs_in_ref),
        (0, rows_ref, q_ref, do_ref, held_ref, dprobs_ref),
    )
    for unit, target, q_side, do_side, held_side, dprobs_side in sides:
        first = unit * tokens
        before = 2 * pair - first
        reach = held_side.shape[1]
        for g in range(kv_heads):
            at = (g * HEAD_SIZE, kv_width + g * HEAD_SIZE)
            top, inverse = norm_ref[unit, g, 0:1], norm_ref[unit, g, 1:2]
            probs = jnp.exp2(held_side[g] - top) * inverse
            dscores = (probs * dprobs_side[g]).astype(jnp.bfloat16)
            keys = window_ref[first:, at[0] : at[0] + HEAD_SIZE]
            own_keys = own_ref[:reach, at[0] : at[0] + HEAD_SIZE]
            dq_t = dot(keys.T, dscores_ref[unit, g, :before]) + dot(own_keys.T, dscores)
            dq = (dq_t * scale).astype(jnp.bfloat16).T
            for a in range(group):
                column = (g * group + a) * HEAD_SIZE
                target[:, column : column + HEAD_SIZE] = dq[a * tokens : (a + 1) * tokens]
            if unit == 0 and g == kv_heads - 1:
                store.start()
            for part, column in (
                (dot(dscores, q_side[g]) * scale, at[0]),
                (dot(probs.astype(jnp.bfloat16), do_side[g]), at[1]),
            ):
                columns = slice(column, column + HEAD_SIZE)
                if unit == 1:
                    own_part_ref[:, columns] = part
                else:
                    own_part_ref[:reach, columns] += part
    store.wait()


def store_kernel(
    core_ref, rows_ref, kept_ref, given_ref, held_ref, dq_ref, key_ref, value_ref, sems
):
    core = core_ref[0]
    width = key_ref.shape[-1]
    copies = [pltpu.make_async_copy(rows_ref, dq_ref.at[1 - core], sems.at[0, 0])]
    for n, (source, slot) in enumerate(((kept_ref, core), (given_ref, 1 - core))):
        for m, target in enumerate((key_ref, value_ref)):
            copies.append(
                pltpu.make_async_copy(
                    source.at[:, pl.ds(m * width, width)], target.at[slot], sems.at[n + 1, m]
                )
            )
    for copy in copies:
        copy.start()
    for copy in copies:
        copy.wait()


def shards(query, key, value, out_grad, attn_out, doc_start):
    count = lax.axis_size("ctx")
    index = lax.axis_index("ctx")
    _, slots, tokens, width = query.shape
    kv_width = key.shape[-1]
    pair_width = 2 * kv_width
    pair = 2 * tokens
    core = (index % 2).astype(jnp.int32)
    stage = jnp.where(core == 0, index // 2, count - 1 - index // 2).astype(jnp.int32)
    core = core[None]
    place = jnp.stack([core[0], stage * pair])
    holder = [2 * s if 2 * s < count else 2 * count - 1 - 2 * s for s in range(count)]
    swap = [(i, i ^ 1) for i in range(count)]

    def shift(x, by):
        moves = [
            (holder[s], holder[s + by]) for s in range(count) if 0 <= s + by < count
        ]
        return lax.ppermute(x, "ctx", moves)

    bf16 = jnp.bfloat16
    def work(flops, moved):
        return pl.CostEstimate(flops=flops, bytes_accessed=moved, transcendentals=0)

    def swapped(x):
        return lax.ppermute(x, "ctx", swap)

    def mine(x):
        return jnp.where(core == 0, x[0], x[1])

    starts_in, key_in, value_in = (swapped(x[0]) for x in (doc_start, key, value))
    sides = ((key[0], value[0]), (key_in, value_in))
    own = jnp.concatenate(
        [jnp.concatenate([mine(x) for x in side], axis=-1) for side in sides], axis=0
    )
    own, starts_in, starts, *late = lax.optimization_barrier(
        (own, starts_in, doc_start[0], query[0], out_grad[0], attn_out[0])
    )
    kv_heads = kv_width // HEAD_SIZE
    lanes = tokens * (width // kv_width)
    products = 2 * slots * tokens * pair * width

    def arranged(unit, starts, sources):
        stacked = jax.ShapeDtypeStruct((kv_heads, lanes, HEAD_SIZE), bf16)
        square = jax.ShapeDtypeStruct((kv_heads, (unit + 1) * tokens, lanes), jnp.float32)
        q, do, scores, dprobs, delta = pl.pallas_call(
            functools.partial(rows_kernel, unit),
            out_shape=(
                stacked,
                stacked,
                square,
                square,
                jax.ShapeDtypeStruct((kv_heads, 8, lanes), jnp.float32),
            ),
            in_specs=[SMEM] + [VMEM] * 5,
            out_specs=(VMEM,) * 5,
            compiler_params=SMALL,
            cost_estimate=work(products // 2, 4 * 2**20),
            name="rows",
        )(place, starts, own, *sources)
        return (starts, q, do, scores, delta), (q, do, scores, dprobs)

    sent = [swapped(x) for x in late]
    far = shift(own, 2)
    near = shift(own, 1)
    side_in = arranged(1, starts_in, sent)
    *late, _ = lax.optimization_barrier((starts, *late, side_in[0][-1]))
    side = arranged(0, late[0], late[1:])
    far_part, near_part, dscores, norm = pl.pallas_call(
        scores_kernel,
        out_shape=(
            jax.ShapeDtypeStruct((pair, pair_width), bf16),
            jax.ShapeDtypeStruct((pair, pair_width), bf16),
            jax.ShapeDtypeStruct((slots, kv_heads, 2 * pair, lanes), bf16),
            jax.ShapeDtypeStruct((slots, kv_heads, 8, lanes), jnp.float32),
        ),
        in_specs=[SMEM] + [VMEM] * 12,
        out_specs=(VMEM,) * 4,
        scratch_shapes=[
            pltpu.VMEM((2 * pair, pair_width), bf16),
            pltpu.VMEM((2 * pair, pair_width), jnp.float32),
        ],
        compiler_params=PARAMS,
        cost_estimate=work(6 * products, 12 * 2**20),
        name="scores",
    )(place, *side[0], *side_in[0], far, near)
    from_far = shift(far_part, -2)
    from_near = shift(near_part, -1)
    dq, dq_send, own_part = pl.pallas_call(
        rest_kernel,
        out_shape=(
            jax.ShapeDtypeStruct((slots, tokens, width), bf16),
            jax.ShapeDtypeStruct((tokens, width), bf16),
            jax.ShapeDtypeStruct((pair, pair_width), jnp.float32),
        ),
        in_specs=[SMEM] + [VMEM] * 13,
        out_specs=(HBM, VMEM, VMEM),
        scratch_shapes=[
            pltpu.VMEM((2 * pair, kv_width), bf16),
            pltpu.VMEM((tokens, width), bf16),
            pltpu.SemaphoreType.DMA,
        ],
        compiler_params=PARAMS,
        cost_estimate=work(3 * products, 8 * 2**20),
        name="rest",
    )(place, *side[1], *side_in[1], far, near, own, dscores, norm)
    dq_rows = swapped(dq_send)
    total = own_part + from_near.astype(jnp.float32) + from_far.astype(jnp.float32)
    total = total.astype(bf16)
    kept = total[:tokens]
    given = swapped(total[tokens:])
    dq, dk, dv = pl.pallas_call(
        store_kernel,
        out_shape=(
            jax.ShapeDtypeStruct(dq.shape, bf16),
            jax.ShapeDtypeStruct((slots, tokens, kv_width), bf16),
            jax.ShapeDtypeStruct((slots, tokens, kv_width), bf16),
        ),
        in_specs=[SMEM, VMEM, VMEM, VMEM, HBM],
        out_specs=(HBM,) * 3,
        scratch_shapes=[pltpu.SemaphoreType.DMA((3, 2))],
        input_output_aliases={4: 0},
        compiler_params=SMALL,
        name="store",
    )(core, dq_rows, kept, given, dq)
    return dq[None], dk[None], dv[None]


def solution(mesh):
    placed = (P("ctx", "dp", None, None),) * 5 + (P("ctx", "dp", None),)
    return jax.shard_map(
        shards,
        mesh=mesh,
        in_specs=placed,
        out_specs=(P("ctx", "dp", None, None),) * 3,
        check_vma=False,
    )
```

```python
import functools

import jax
import jax.numpy as jnp
from jax import lax
from jax.experimental import pallas as pl
from jax.experimental.pallas import tpu as pltpu
from jax.sharding import PartitionSpec as P

HEAD_SIZE = 128
STEPS = 4
LOG2E = 1.4426950408889634
CONTRACT_LAST = (((1,), (1,)), ((), ()))
CONTRACT_ROWS = (((1,), (0,)), ((), ()))
VMEM = pl.BlockSpec(memory_space=pltpu.VMEM)
SMEM = pl.BlockSpec(memory_space=pltpu.SMEM)
HBM = pl.BlockSpec(memory_space=pltpu.HBM)
PARAMS = pltpu.CompilerParams(vmem_limit_bytes=24 * 2**20)
SMALL = pltpu.CompilerParams(vmem_limit_bytes=4 * 2**20)


def dot(a, b, dims=CONTRACT_ROWS):
    return lax.dot_general(a, b, dims, preferred_element_type=jnp.float32)


def stack_heads(ref, first, count):
    return jnp.concatenate(
        [ref[:, (first + a) * HEAD_SIZE : (first + a + 1) * HEAD_SIZE] for a in range(count)],
        axis=0,
    )


def unit_starts(starts_ref, core):
    return jnp.where(core == 0, starts_ref[0:1, :], starts_ref[1:2, :])


def rows_kernel(
    unit, place_ref, starts_ref, own_ref, q_ref, do_ref, o_ref,
    q_out_ref, do_out_ref, scores_ref, dprobs_ref, delta_ref,
):
    core, begin = place_ref[0], place_ref[1]
    tokens = q_ref.shape[1]
    kv_heads, reach, lanes = scores_ref.shape
    kv_width = kv_heads * HEAD_SIZE
    group = lanes // tokens
    factor = HEAD_SIZE ** (-0.5) * LOG2E
    ones = jnp.ones((delta_ref.shape[1], 2 * HEAD_SIZE), jnp.bfloat16)
    low = unit_starts(starts_ref, core) - begin
    high = lax.broadcasted_iota(jnp.int32, (1, tokens), 1) + unit * tokens
    row = lax.broadcasted_iota(jnp.int32, (reach, tokens), 0)
    bias = jnp.where((row >= low) & (row <= high), 0.0, -jnp.inf)
    bias = jnp.concatenate([bias] * group, axis=1)
    for g in range(kv_heads):
        q, do, o = (
            stack_heads(r.at[core], g * group, group) for r in (q_ref, do_ref, o_ref)
        )
        keys = own_ref[:reach, g * HEAD_SIZE : (g + 1) * HEAD_SIZE]
        values = own_ref[:reach, kv_width + g * HEAD_SIZE : kv_width + (g + 1) * HEAD_SIZE]
        terms = do.astype(jnp.float32) * o.astype(jnp.float32)
        coarse = terms.astype(jnp.bfloat16)
        fine = (terms - coarse.astype(jnp.float32)).astype(jnp.bfloat16)
        delta = dot(ones, jnp.concatenate([coarse, fine], axis=1), CONTRACT_LAST)
        delta_ref[g] = delta
        scores_ref[g] = dot(keys, q, CONTRACT_LAST) * factor + bias
        dprobs_ref[g] = dot(values, do, CONTRACT_LAST) - delta[:1]
        q_out_ref[g] = q
        do_out_ref[g] = do


def scores_kernel(
    place_ref, starts_ref, q_ref, do_ref, held_ref, delta_ref,
    starts_in_ref, q_in_ref, do_in_ref, held_in_ref, delta_in_ref, far_ref, near_ref,
    far_part_ref, near_part_ref, dscores_ref, norm_ref, window_ref, part_ref,
):
    core, begin = place_ref[0], place_ref[1]
    tokens = starts_ref.shape[1]
    kv_heads, lanes = q_ref.shape[:2]
    kv_width = kv_heads * HEAD_SIZE
    group = lanes // tokens
    scale = HEAD_SIZE ** (-0.5)
    pair = 2 * tokens
    for n, source in enumerate((far_ref, near_ref)):
        window_ref[n * pair : (n + 1) * pair, :] = source[...]
    offset = lax.broadcasted_iota(jnp.int32, (1, tokens), 1)
    sides = (
        (starts_ref, q_ref, do_ref, held_ref, delta_ref),
        (starts_in_ref, q_in_ref, do_in_ref, held_in_ref, delta_in_ref),
    )

    def products(unit, g):
        starts, q_side, do_side, held_side, delta_side = sides[unit]
        first = unit * tokens
        columns = slice(g * HEAD_SIZE, (g + 1) * HEAD_SIZE)
        values = window_ref[first:, kv_width + g * HEAD_SIZE : kv_width + (g + 1) * HEAD_SIZE]
        low = unit_starts(starts, core) - (begin + (unit - STEPS) * tokens)
        low = jnp.concatenate([jnp.maximum(offset + 1, low)] * group, axis=1)
        scores = dot(window_ref[first:, columns], q_side[g], CONTRACT_LAST) * (scale * LOG2E)
        row = lax.broadcasted_iota(jnp.int32, scores.shape, 0)
        scores = jnp.where(row >= low, scores, -jnp.inf)
        return scores, dot(values, do_side[g], CONTRACT_LAST)

    order = [(unit, g) for unit in range(2) for g in range(kv_heads)]
    ahead = products(*order[0])
    for step, (unit, g) in enumerate(order):
        scores, dprobs = ahead
        if step + 1 < len(order):
            ahead = products(*order[step + 1])
        _, q_side, do_side, held_side, delta_side = sides[unit]
        first = unit * tokens
        before = 2 * pair - first
        held = held_side[g]
        top = jnp.maximum(
            jnp.max(scores, axis=0, keepdims=True), jnp.max(held, axis=0, keepdims=True)
        )
        weights = jnp.exp2(scores - top)
        total = jnp.sum(weights, axis=0, keepdims=True)
        total += jnp.sum(jnp.exp2(held - top), axis=0, keepdims=True)
        inverse = 1.0 / total
        probs = weights * inverse
        norm_ref[unit, g, 0:1] = top
        norm_ref[unit, g, 1:2] = inverse
        dscores = (probs * (dprobs - delta_side[g, :1])).astype(jnp.bfloat16)
        dscores_ref[unit, g, :before] = dscores
        for part, column in (
            (dot(dscores, q_side[g]) * scale, g * HEAD_SIZE),
            (dot(probs.astype(jnp.bfloat16), do_side[g]), kv_width + g * HEAD_SIZE),
        ):
            columns = slice(column, column + HEAD_SIZE)
            if unit == 0:
                part_ref[:, columns] = part
            else:
                part_ref[first:, columns] += part
    far_part_ref[...] = part_ref[:pair, :].astype(jnp.bfloat16)
    near_part_ref[...] = part_ref[pair:, :].astype(jnp.bfloat16)


def rest_kernel(
    place_ref, q_ref, do_ref, held_ref, dprobs_ref, q_in_ref, do_in_ref, held_in_ref,
    dprobs_in_ref, far_ref, near_ref, own_ref, dscores_ref, norm_ref,
    dq_ref, dq_send_ref, own_part_ref, window_ref, rows_ref, sem,
):
    core = place_ref[0]
    tokens = dq_send_ref.shape[0]
    kv_heads, lanes = q_ref.shape[:2]
    kv_width = kv_heads * HEAD_SIZE
    group = lanes // tokens
    scale = HEAD_SIZE ** (-0.5)
    pair = 2 * tokens
    for n, source in enumerate((far_ref, near_ref)):
        window_ref[n * pair : (n + 1) * pair, :] = source[:, :kv_width]
    store = pltpu.make_async_copy(rows_ref, dq_ref.at[core], sem)
    sides = (
        (1, dq_send_ref, q_in_ref, do_in_ref, held_in_ref, dprobs_in_ref),
        (0, rows_ref, q_ref, do_ref, held_ref, dprobs_ref),
    )
    for unit, target, q_side, do_side, held_side, dprobs_side in sides:
        first = unit * tokens
        before = 2 * pair - first
        reach = held_side.shape[1]
        for g in range(kv_heads):
            at = (g * HEAD_SIZE, kv_width + g * HEAD_SIZE)
            top, inverse = norm_ref[unit, g, 0:1], norm_ref[unit, g, 1:2]
            probs = jnp.exp2(held_side[g] - top) * inverse
            dscores = (probs * dprobs_side[g]).astype(jnp.bfloat16)
            keys = window_ref[first:, at[0] : at[0] + HEAD_SIZE]
            own_keys = own_ref[:reach, at[0] : at[0] + HEAD_SIZE]
            dq_t = dot(keys.T, dscores_ref[unit, g, :before]) + dot(own_keys.T, dscores)
            dq = (dq_t * scale).astype(jnp.bfloat16).T
            for a in range(group):
                column = (g * group + a) * HEAD_SIZE
                target[:, column : column + HEAD_SIZE] = dq[a * tokens : (a + 1) * tokens]
            if unit == 0 and g == kv_heads - 1:
                store.start()
            for part, column in (
                (dot(dscores, q_side[g]) * scale, at[0]),
                (dot(probs.astype(jnp.bfloat16), do_side[g]), at[1]),
            ):
                columns = slice(column, column + HEAD_SIZE)
                if unit == 1:
                    own_part_ref[:, columns] = part
                else:
                    own_part_ref[:reach, columns] += part
    store.wait()


def store_kernel(
    core_ref, rows_ref, kept_ref, given_ref, held_ref, dq_ref, key_ref, value_ref, sems
):
    core = core_ref[0]
    width = key_ref.shape[-1]
    copies = [pltpu.make_async_copy(rows_ref, dq_ref.at[1 - core], sems.at[0, 0])]
    for n, (source, slot) in enumerate(((kept_ref, core), (given_ref, 1 - core))):
        for m, target in enumerate((key_ref, value_ref)):
            copies.append(
                pltpu.make_async_copy(
                    source.at[:, pl.ds(m * width, width)], target.at[slot], sems.at[n + 1, m]
                )
            )
    for copy in copies:
        copy.start()
    for copy in copies:
        copy.wait()


def shards(query, key, value, out_grad, attn_out, doc_start):
    count = lax.axis_size("ctx")
    index = lax.axis_index("ctx")
    _, slots, tokens, width = query.shape
    kv_width = key.shape[-1]
    pair_width = 2 * kv_width
    pair = 2 * tokens
    core = (index % 2).astype(jnp.int32)
    stage = jnp.where(core == 0, index // 2, count - 1 - index // 2).astype(jnp.int32)
    core = core[None]
    place = jnp.stack([core[0], stage * pair])
    holder = [2 * s if 2 * s < count else 2 * count - 1 - 2 * s for s in range(count)]
    swap = [(i, i ^ 1) for i in range(count)]

    def shift(x, by):
        moves = [
            (holder[s], holder[s + by]) for s in range(count) if 0 <= s + by < count
        ]
        return lax.ppermute(x, "ctx", moves)

    bf16 = jnp.bfloat16
    def work(flops, moved):
        return pl.CostEstimate(flops=flops, bytes_accessed=moved, transcendentals=0)

    def swapped(x):
        return lax.ppermute(x, "ctx", swap)

    def mine(x):
        return jnp.where(core == 0, x[0], x[1])

    key_in, value_in = swapped(key[0]), swapped(value[0])
    keep, starts = lax.optimization_barrier(
        (jnp.concatenate([mine(key[0]), mine(value[0])], axis=-1), doc_start[0])
    )
    starts_in = swapped(starts)
    given = jnp.concatenate([mine(key_in), mine(value_in)], axis=-1)
    own = jnp.concatenate([keep, given], axis=0)
    own, *late = lax.optimization_barrier((own, query[0], out_grad[0], attn_out[0]))
    kv_heads = kv_width // HEAD_SIZE
    lanes = tokens * (width // kv_width)
    products = 2 * slots * tokens * pair * width

    def arranged(unit, starts, sources):
        stacked = jax.ShapeDtypeStruct((kv_heads, lanes, HEAD_SIZE), bf16)
        square = jax.ShapeDtypeStruct((kv_heads, (unit + 1) * tokens, lanes), jnp.float32)
        q, do, scores, dprobs, delta = pl.pallas_call(
            functools.partial(rows_kernel, unit),
            out_shape=(
                stacked,
                stacked,
                square,
                square,
                jax.ShapeDtypeStruct((kv_heads, 8, lanes), jnp.float32),
            ),
            in_specs=[SMEM] + [VMEM] * 5,
            out_specs=(VMEM,) * 5,
            compiler_params=SMALL,
            cost_estimate=work(products // 2, 4 * 2**20),
            name="rows",
        )(place, starts, own, *sources)
        return (starts, q, do, scores, delta), (q, do, scores, dprobs)

    sent = [swapped(x) for x in late]
    far = shift(own, 2)
    near = shift(own, 1)
    side_in = arranged(1, starts_in, sent)
    *late, _ = lax.optimization_barrier((starts, *late, side_in[0][-1]))
    side = arranged(0, late[0], late[1:])
    far_part, near_part, dscores, norm = pl.pallas_call(
        scores_kernel,
        out_shape=(
            jax.ShapeDtypeStruct((pair, pair_width), bf16),
            jax.ShapeDtypeStruct((pair, pair_width), bf16),
            jax.ShapeDtypeStruct((slots, kv_heads, 2 * pair, lanes), bf16),
            jax.ShapeDtypeStruct((slots, kv_heads, 8, lanes), jnp.float32),
        ),
        in_specs=[SMEM] + [VMEM] * 12,
        out_specs=(VMEM,) * 4,
        scratch_shapes=[
            pltpu.VMEM((2 * pair, pair_width), bf16),
            pltpu.VMEM((2 * pair, pair_width), jnp.float32),
        ],
        compiler_params=PARAMS,
        cost_estimate=work(6 * products, 12 * 2**20),
        name="scores",
    )(place, *side[0], *side_in[0], far, near)
    from_far = shift(far_part, -2)
    from_near = shift(near_part, -1)
    dq, dq_send, own_part = pl.pallas_call(
        rest_kernel,
        out_shape=(
            jax.ShapeDtypeStruct((slots, tokens, width), bf16),
            jax.ShapeDtypeStruct((tokens, width), bf16),
            jax.ShapeDtypeStruct((pair, pair_width), jnp.float32),
        ),
        in_specs=[SMEM] + [VMEM] * 13,
        out_specs=(HBM, VMEM, VMEM),
        scratch_shapes=[
            pltpu.VMEM((2 * pair, kv_width), bf16),
            pltpu.VMEM((tokens, width), bf16),
            pltpu.SemaphoreType.DMA,
        ],
        compiler_params=PARAMS,
        cost_estimate=work(3 * products, 8 * 2**20),
        name="rest",
    )(place, *side[1], *side_in[1], far, near, own, dscores, norm)
    dq_rows = swapped(dq_send)
    total = own_part + from_near.astype(jnp.float32) + from_far.astype(jnp.float32)
    total = total.astype(bf16)
    kept = total[:tokens]
    given = swapped(total[tokens:])
    dq, dk, dv = pl.pallas_call(
        store_kernel,
        out_shape=(
            jax.ShapeDtypeStruct(dq.shape, bf16),
            jax.ShapeDtypeStruct((slots, tokens, kv_width), bf16),
            jax.ShapeDtypeStruct((slots, tokens, kv_width), bf16),
        ),
        in_specs=[SMEM, VMEM, VMEM, VMEM, HBM],
        out_specs=(HBM,) * 3,
        scratch_shapes=[pltpu.SemaphoreType.DMA((3, 2))],
        input_output_aliases={4: 0},
        compiler_params=SMALL,
        name="store",
    )(core, dq_rows, kept, given, dq)
    return dq[None], dk[None], dv[None]


def solution(mesh):
    placed = (P("ctx", "dp", None, None),) * 5 + (P("ctx", "dp", None),)
    return jax.shard_map(
        shards,
        mesh=mesh,
        in_specs=placed,
        out_specs=(P("ctx", "dp", None, None),) * 3,
        check_vma=False,
    )
```

```python
import functools

import jax
import jax.numpy as jnp
from jax import lax
from jax.experimental import pallas as pl
from jax.experimental.pallas import tpu as pltpu
from jax.sharding import PartitionSpec as P

HEAD_SIZE = 128
STEPS = 4
LOG2E = 1.4426950408889634
CONTRACT_LAST = (((1,), (1,)), ((), ()))
CONTRACT_ROWS = (((1,), (0,)), ((), ()))
VMEM = pl.BlockSpec(memory_space=pltpu.VMEM)
SMEM = pl.BlockSpec(memory_space=pltpu.SMEM)
HBM = pl.BlockSpec(memory_space=pltpu.HBM)
PARAMS = pltpu.CompilerParams(vmem_limit_bytes=24 * 2**20)
SMALL = pltpu.CompilerParams(vmem_limit_bytes=4 * 2**20)


def dot(a, b, dims=CONTRACT_ROWS):
    return lax.dot_general(a, b, dims, preferred_element_type=jnp.float32)


def stack_heads(ref, first, count):
    return jnp.concatenate(
        [ref[:, (first + a) * HEAD_SIZE : (first + a + 1) * HEAD_SIZE] for a in range(count)],
        axis=0,
    )


def unit_starts(starts_ref, core):
    return jnp.where(core == 0, starts_ref[0:1, :], starts_ref[1:2, :])


def rows_kernel(
    unit, place_ref, starts_ref, own_ref, q_ref, do_ref, o_ref,
    q_out_ref, do_out_ref, scores_ref, dprobs_ref, delta_ref,
):
    core, begin = place_ref[0], place_ref[1]
    tokens = q_ref.shape[1]
    kv_heads, reach, lanes = scores_ref.shape
    kv_width = kv_heads * HEAD_SIZE
    group = lanes // tokens
    factor = HEAD_SIZE ** (-0.5) * LOG2E
    ones = jnp.ones((delta_ref.shape[1], 2 * HEAD_SIZE), jnp.bfloat16)
    low = unit_starts(starts_ref, core) - begin
    high = lax.broadcasted_iota(jnp.int32, (1, tokens), 1) + unit * tokens
    row = lax.broadcasted_iota(jnp.int32, (reach, tokens), 0)
    bias = jnp.where((row >= low) & (row <= high), 0.0, -jnp.inf)
    bias = jnp.concatenate([bias] * group, axis=1)
    for g in range(kv_heads):
        q, do, o = (
            stack_heads(r.at[core], g * group, group) for r in (q_ref, do_ref, o_ref)
        )
        keys = own_ref[:reach, g * HEAD_SIZE : (g + 1) * HEAD_SIZE]
        values = own_ref[:reach, kv_width + g * HEAD_SIZE : kv_width + (g + 1) * HEAD_SIZE]
        terms = do.astype(jnp.float32) * o.astype(jnp.float32)
        coarse = terms.astype(jnp.bfloat16)
        fine = (terms - coarse.astype(jnp.float32)).astype(jnp.bfloat16)
        delta = dot(ones, jnp.concatenate([coarse, fine], axis=1), CONTRACT_LAST)
        delta_ref[g] = delta
        scores_ref[g] = dot(keys, q, CONTRACT_LAST) * factor + bias
        dprobs_ref[g] = dot(values, do, CONTRACT_LAST) - delta[:1]
        q_out_ref[g] = q
        do_out_ref[g] = do


def scores_kernel(
    place_ref, starts_ref, q_ref, do_ref, held_ref, delta_ref,
    starts_in_ref, q_in_ref, do_in_ref, held_in_ref, delta_in_ref, far_ref, near_ref,
    far_part_ref, near_part_ref, dscores_ref, norm_ref, window_ref, part_ref,
):
    core, begin = place_ref[0], place_ref[1]
    tokens = starts_ref.shape[1]
    kv_heads, lanes = q_ref.shape[:2]
    kv_width = kv_heads * HEAD_SIZE
    group = lanes // tokens
    scale = HEAD_SIZE ** (-0.5)
    pair = 2 * tokens
    for n, source in enumerate((far_ref, near_ref)):
        window_ref[n * pair : (n + 1) * pair, :] = source[...]
    offset = lax.broadcasted_iota(jnp.int32, (1, tokens), 1)
    sides = (
        (starts_ref, q_ref, do_ref, held_ref, delta_ref),
        (starts_in_ref, q_in_ref, do_in_ref, held_in_ref, delta_in_ref),
    )

    def products(unit, g):
        starts, q_side, do_side, held_side, delta_side = sides[unit]
        first = unit * tokens
        columns = slice(g * HEAD_SIZE, (g + 1) * HEAD_SIZE)
        values = window_ref[first:, kv_width + g * HEAD_SIZE : kv_width + (g + 1) * HEAD_SIZE]
        low = unit_starts(starts, core) - (begin + (unit - STEPS) * tokens)
        low = jnp.concatenate([jnp.maximum(offset + 1, low)] * group, axis=1)
        scores = dot(window_ref[first:, columns], q_side[g], CONTRACT_LAST) * (scale * LOG2E)
        row = lax.broadcasted_iota(jnp.int32, scores.shape, 0)
        scores = jnp.where(row >= low, scores, -jnp.inf)
        return scores, dot(values, do_side[g], CONTRACT_LAST)

    order = [(unit, g) for unit in range(2) for g in range(kv_heads)]
    ahead = [products(*item) for item in order[:2]]
    for step, (unit, g) in enumerate(order):
        scores, dprobs = ahead.pop(0)
        if step + 2 < len(order):
            ahead.append(products(*order[step + 2]))
        _, q_side, do_side, held_side, delta_side = sides[unit]
        first = unit * tokens
        before = 2 * pair - first
        held = held_side[g]
        top = jnp.maximum(
            jnp.max(scores, axis=0, keepdims=True), jnp.max(held, axis=0, keepdims=True)
        )
        weights = jnp.exp2(scores - top)
        total = jnp.sum(weights, axis=0, keepdims=True)
        total += jnp.sum(jnp.exp2(held - top), axis=0, keepdims=True)
        inverse = 1.0 / total
        probs = weights * inverse
        norm_ref[unit, g, 0:1] = top
        norm_ref[unit, g, 1:2] = inverse
        dscores = (probs * (dprobs - delta_side[g, :1])).astype(jnp.bfloat16)
        dscores_ref[unit, g, :before] = dscores
        for part, column in (
            (dot(dscores, q_side[g]), g * HEAD_SIZE),
            (dot(probs.astype(jnp.bfloat16), do_side[g]), kv_width + g * HEAD_SIZE),
        ):
            columns = slice(column, column + HEAD_SIZE)
            if unit == 0:
                part_ref[:, columns] = part
            else:
                part_ref[first:, columns] += part
    part_ref[:, :kv_width] *= scale
    far_part_ref[...] = part_ref[:pair, :].astype(jnp.bfloat16)
    near_part_ref[...] = part_ref[pair:, :].astype(jnp.bfloat16)


def rest_kernel(
    place_ref, q_ref, do_ref, held_ref, dprobs_ref, q_in_ref, do_in_ref, held_in_ref,
    dprobs_in_ref, far_ref, near_ref, own_ref, dscores_ref, norm_ref,
    dq_ref, dq_send_ref, own_part_ref, window_ref, rows_ref, sem,
):
    core = place_ref[0]
    tokens = dq_send_ref.shape[0]
    kv_heads, lanes = q_ref.shape[:2]
    kv_width = kv_heads * HEAD_SIZE
    group = lanes // tokens
    scale = HEAD_SIZE ** (-0.5)
    pair = 2 * tokens
    for n, source in enumerate((far_ref, near_ref)):
        window_ref[n * pair : (n + 1) * pair, :] = source[:, :kv_width]
    store = pltpu.make_async_copy(rows_ref, dq_ref.at[core], sem)
    sides = (
        (1, dq_send_ref, q_in_ref, do_in_ref, held_in_ref, dprobs_in_ref),
        (0, rows_ref, q_ref, do_ref, held_ref, dprobs_ref),
    )
    for unit, target, q_side, do_side, held_side, dprobs_side in sides:
        first = unit * tokens
        before = 2 * pair - first
        reach = held_side.shape[1]
        for g in range(kv_heads):
            at = (g * HEAD_SIZE, kv_width + g * HEAD_SIZE)
            top, inverse = norm_ref[unit, g, 0:1], norm_ref[unit, g, 1:2]
            probs = jnp.exp2(held_side[g] - top) * inverse
            dscores = (probs * dprobs_side[g]).astype(jnp.bfloat16)
            keys = window_ref[first:, at[0] : at[0] + HEAD_SIZE]
            own_keys = own_ref[:reach, at[0] : at[0] + HEAD_SIZE]
            dq_t = dot(keys.T, dscores_ref[unit, g, :before]) + dot(own_keys.T, dscores)
            dq = (dq_t * scale).astype(jnp.bfloat16).T
            for a in range(group):
                column = (g * group + a) * HEAD_SIZE
                target[:, column : column + HEAD_SIZE] = dq[a * tokens : (a + 1) * tokens]
            if unit == 0 and g == kv_heads - 1:
                store.start()
            for part, column in (
                (dot(dscores, q_side[g]) * scale, at[0]),
                (dot(probs.astype(jnp.bfloat16), do_side[g]), at[1]),
            ):
                columns = slice(column, column + HEAD_SIZE)
                if unit == 1:
                    own_part_ref[:, columns] = part
                else:
                    own_part_ref[:reach, columns] += part
    store.wait()


def store_kernel(
    core_ref, rows_ref, kept_ref, given_ref, held_ref, dq_ref, key_ref, value_ref, sems
):
    core = core_ref[0]
    width = key_ref.shape[-1]
    copies = [pltpu.make_async_copy(rows_ref, dq_ref.at[1 - core], sems.at[0, 0])]
    for n, (source, slot) in enumerate(((kept_ref, core), (given_ref, 1 - core))):
        for m, target in enumerate((key_ref, value_ref)):
            copies.append(
                pltpu.make_async_copy(
                    source.at[:, pl.ds(m * width, width)], target.at[slot], sems.at[n + 1, m]
                )
            )
    for copy in copies:
        copy.start()
    for copy in copies:
        copy.wait()


def shards(query, key, value, out_grad, attn_out, doc_start):
    count = lax.axis_size("ctx")
    index = lax.axis_index("ctx")
    _, slots, tokens, width = query.shape
    kv_width = key.shape[-1]
    pair_width = 2 * kv_width
    pair = 2 * tokens
    core = (index % 2).astype(jnp.int32)
    stage = jnp.where(core == 0, index // 2, count - 1 - index // 2).astype(jnp.int32)
    core = core[None]
    place = jnp.stack([core[0], stage * pair])
    holder = [2 * s if 2 * s < count else 2 * count - 1 - 2 * s for s in range(count)]
    swap = [(i, i ^ 1) for i in range(count)]

    def shift(x, by):
        moves = [
            (holder[s], holder[s + by]) for s in range(count) if 0 <= s + by < count
        ]
        return lax.ppermute(x, "ctx", moves)

    bf16 = jnp.bfloat16
    def work(flops, moved):
        return pl.CostEstimate(flops=flops, bytes_accessed=moved, transcendentals=0)

    def swapped(x):
        return lax.ppermute(x, "ctx", swap)

    def mine(x):
        return jnp.where(core == 0, x[0], x[1])

    key_in, value_in = swapped(key[0]), swapped(value[0])
    keep, starts = lax.optimization_barrier(
        (jnp.concatenate([mine(key[0]), mine(value[0])], axis=-1), doc_start[0])
    )
    starts_in = swapped(starts)
    given = jnp.concatenate([mine(key_in), mine(value_in)], axis=-1)
    own = jnp.concatenate([keep, given], axis=0)
    own, *late = lax.optimization_barrier((own, query[0], out_grad[0], attn_out[0]))
    kv_heads = kv_width // HEAD_SIZE
    lanes = tokens * (width // kv_width)
    products = 2 * slots * tokens * pair * width

    def arranged(unit, starts, sources):
        stacked = jax.ShapeDtypeStruct((kv_heads, lanes, HEAD_SIZE), bf16)
        square = jax.ShapeDtypeStruct((kv_heads, (unit + 1) * tokens, lanes), jnp.float32)
        q, do, scores, dprobs, delta = pl.pallas_call(
            functools.partial(rows_kernel, unit),
            out_shape=(
                stacked,
                stacked,
                square,
                square,
                jax.ShapeDtypeStruct((kv_heads, 8, lanes), jnp.float32),
            ),
            in_specs=[SMEM] + [VMEM] * 5,
            out_specs=(VMEM,) * 5,
            compiler_params=SMALL,
            cost_estimate=work(products // 2, 4 * 2**20),
            name="rows",
        )(place, starts, own, *sources)
        return (starts, q, do, scores, delta), (q, do, scores, dprobs)

    sent = [swapped(x) for x in late]
    far = shift(own, 2)
    near = shift(own, 1)
    side_in = arranged(1, starts_in, sent)
    *late, _ = lax.optimization_barrier((starts, *late, side_in[0][-1]))
    side = arranged(0, late[0], late[1:])
    far_part, near_part, dscores, norm = pl.pallas_call(
        scores_kernel,
        out_shape=(
            jax.ShapeDtypeStruct((pair, pair_width), bf16),
            jax.ShapeDtypeStruct((pair, pair_width), bf16),
            jax.ShapeDtypeStruct((slots, kv_heads, 2 * pair, lanes), bf16),
            jax.ShapeDtypeStruct((slots, kv_heads, 8, lanes), jnp.float32),
        ),
        in_specs=[SMEM] + [VMEM] * 12,
        out_specs=(VMEM,) * 4,
        scratch_shapes=[
            pltpu.VMEM((2 * pair, pair_width), bf16),
            pltpu.VMEM((2 * pair, pair_width), jnp.float32),
        ],
        compiler_params=PARAMS,
        cost_estimate=work(6 * products, 12 * 2**20),
        name="scores",
    )(place, *side[0], *side_in[0], far, near)
    from_far = shift(far_part, -2)
    from_near = shift(near_part, -1)
    dq, dq_send, own_part = pl.pallas_call(
        rest_kernel,
        out_shape=(
            jax.ShapeDtypeStruct((slots, tokens, width), bf16),
            jax.ShapeDtypeStruct((tokens, width), bf16),
            jax.ShapeDtypeStruct((pair, pair_width), jnp.float32),
        ),
        in_specs=[SMEM] + [VMEM] * 13,
        out_specs=(HBM, VMEM, VMEM),
        scratch_shapes=[
            pltpu.VMEM((2 * pair, kv_width), bf16),
            pltpu.VMEM((tokens, width), bf16),
            pltpu.SemaphoreType.DMA,
        ],
        compiler_params=PARAMS,
        cost_estimate=work(3 * products, 8 * 2**20),
        name="rest",
    )(place, *side[1], *side_in[1], far, near, own, dscores, norm)
    dq_rows = swapped(dq_send)
    total = own_part + from_near.astype(jnp.float32) + from_far.astype(jnp.float32)
    total = total.astype(bf16)
    kept = total[:tokens]
    given = swapped(total[tokens:])
    dq, dk, dv = pl.pallas_call(
        store_kernel,
        out_shape=(
            jax.ShapeDtypeStruct(dq.shape, bf16),
            jax.ShapeDtypeStruct((slots, tokens, kv_width), bf16),
            jax.ShapeDtypeStruct((slots, tokens, kv_width), bf16),
        ),
        in_specs=[SMEM, VMEM, VMEM, VMEM, HBM],
        out_specs=(HBM,) * 3,
        scratch_shapes=[pltpu.SemaphoreType.DMA((3, 2))],
        input_output_aliases={4: 0},
        compiler_params=SMALL,
        name="store",
    )(core, dq_rows, kept, given, dq)
    return dq[None], dk[None], dv[None]


def solution(mesh):
    placed = (P("ctx", "dp", None, None),) * 5 + (P("ctx", "dp", None),)
    return jax.shard_map(
        shards,
        mesh=mesh,
        in_specs=placed,
        out_specs=(P("ctx", "dp", None, None),) * 3,
        check_vma=False,
    )
```
